256 devices in a mesh: ctx: 16 (over y, x_lo, core), tp: 16 (over z, x_hi).
Axes of the slice: x: 4 (x_hi: 2, x_lo: 2; x = x_hi * 2 + x_lo), y: 4, z: 8, core: 2. Of those that a mesh axis runs over, the one named last changes fastest.
Arguments:
- residual: bfloat16 [16384, 8192], P('ctx', 'tp'), may hold values from -6 to 6
- queries: bfloat16 [16, 256, 8192], P('ctx', 'tp'), may hold values from -36 to 36
- keys_values: bfloat16 [16, 256, 2048], P('ctx', 'tp'), may hold values from -6 to 6
- kept_local: int32 [16, 256], replicated, may hold values from 0 to 1024, as said below
- router_weight: bfloat16 [16, 256], P('ctx'), may hold values from 0.25 to 1
Outputs:
- layer_out: bfloat16 [16384, 8192], P('ctx', 'tp')
The draws below stay inside these ranges and needn't reach their ends.
Inputs may be any that keep to these rules, and one draw needn't show every extreme that they name: `kept_local`: row j lists in rising order the distinct positions of block j's kept tokens, then 1024 in the remaining slots. All blocks together keep exactly 2048 tokens, every block keeps 2 or more, and some block keeps exactly 256.
All inputs are finite; a program needn't handle non-finite values.
Results may differ from the reference program's by a relative error of at most 0.0011.
Values may be sent and summed in bfloat16 or wider, within the bound.
No kernel may reach another device: no remote copies, remote signals or barrier semaphores. Data moves between devices by JAX's collectives and lax.ppermute only.
A program may use at most 64 MiB of HBM per device.

```python
import math
import jax
import jax.numpy as jnp
from jax import lax

H = 64
KVH = 8
HD = 128
TOK_DEV = 1024
CAP = 256
KEPT = 2048
TOKENS = 16384
N_CTX = 16


def draw_queries(key, part):
    key = jax.random.fold_in(key, 31)
    values = jnp.clip(2.5 * jax.random.normal(key, (N_CTX, CAP, H, HD), jnp.float32), -10.0, 10.0)
    return values.reshape(N_CTX, CAP, H * HD).astype(jnp.bfloat16)


def draw_keys_values(key, part):
    key = jax.random.fold_in(key, 47)
    values = jnp.clip(jax.random.normal(key, (N_CTX, CAP, KVH, 2, HD), jnp.float32), -6.0, 6.0)
    return values.reshape(N_CTX, CAP, 2 * KVH * HD).astype(jnp.bfloat16)


def draw_kept_local(key, part):
    key = jax.random.fold_in(key, 11)
    pick_key, weight_key, order_key = jax.random.split(key, 3)
    busiest = jax.random.randint(pick_key, (), 0, N_CTX)
    blocks = jnp.arange(N_CTX, dtype=jnp.int32)
    others = blocks != busiest
    weights = jnp.where(others, jax.random.randint(weight_key, (N_CTX,), 2, 5), 0).astype(jnp.int32)
    spread = KEPT - CAP
    base_count = weights * spread // jnp.sum(weights)
    leftover = spread - jnp.sum(base_count)
    extra_count = (others & (jnp.cumsum(others.astype(jnp.int32)) <= leftover)).astype(jnp.int32)
    counts = jnp.where(others, base_count + extra_count, CAP).astype(jnp.int32)

    def one_block(block_key, block_count):
        shuffled = jax.random.permutation(block_key, TOK_DEV)
        places = jnp.arange(TOK_DEV, dtype=jnp.int32)
        sort_keys = jnp.where(shuffled < block_count, places, TOK_DEV + places)
        chosen = jnp.sort(sort_keys)[:CAP]
        return jnp.where(chosen < TOK_DEV, chosen, TOK_DEV)
    return jax.vmap(one_block)(jax.random.split(order_key, N_CTX), counts).astype(jnp.int32)


def steps_of(rng, extent, shards, smallest, largest):
    loudness = 1.0
    for dim, shards_of in shards:
        heights = jax.random.uniform(jax.random.fold_in(jax.random.fold_in(rng, 6), dim), (shards_of,), jnp.float32, smallest / len(shards), largest / len(shards))
        loudness = loudness * jnp.repeat(jnp.exp(heights), extent[dim] // shards_of).reshape((-1,) + (1,) * (len(extent) - 1 - dim))
    return loudness


def gaussian(rng, dims, deviation, bound, cuts=(), kind=jnp.bfloat16):
    values = deviation * jax.random.normal(rng, dims, jnp.float32)
    if cuts:
        values = values * steps_of(rng, dims, cuts, -0.22, 0.18)
    return jnp.clip(values, -bound, bound).astype(kind)


def setup_inputs(seed: int = 0) -> dict:
    splits = jax.random.split(jax.random.key(seed), 6)
    return {
        "residual": gaussian(splits[0], (TOKENS, H * HD), 1.0, 6.0, ((0, 16), (1, 16))),
        "queries": draw_queries(jax.random.fold_in(splits[5], 71), 0),
        "keys_values": draw_keys_values(jax.random.fold_in(splits[5], 71), 0),
        "kept_local": draw_kept_local(jax.random.fold_in(splits[5], 71), 0),
        "router_weight": jnp.clip(jnp.exp(math.log(1.0) - 1.3862944 * jax.random.uniform(splits[4], (N_CTX, CAP), jnp.float32) ** steps_of(splits[4], (N_CTX, CAP), ((0, 16),), -0.2, 0.2)), 0.25, 1.0).astype(jnp.bfloat16),
    }


def reference(residual, queries, keys_values, kept_local, router_weight):
    counts = lax.optimization_barrier(jnp.sum((kept_local < TOK_DEV).astype(jnp.int32), axis=1))
    block_ends = jnp.cumsum(counts).astype(jnp.int32)
    starts = block_ends - counts
    ranks = jnp.arange(KEPT, dtype=jnp.int32)
    owner_block = lax.optimization_barrier(jnp.sum((block_ends[None, :] <= ranks[:, None]).astype(jnp.int32), axis=1))
    slot_index = (ranks - starts[owner_block]).astype(jnp.int32)
    query_rows = queries[owner_block, slot_index].reshape(KEPT, H, HD)
    pair_rows = keys_values[owner_block, slot_index].reshape(KEPT, KVH, 2, HD)
    router_rows = router_weight[owner_block, slot_index].astype(jnp.float32)
    causal = ranks[None, :] <= ranks[:, None]
    group_size = H // KVH
    score_scale = 1.0 / math.sqrt(HD)

    def one_head(head_args):
        head_index, query_head = head_args
        pair_head = lax.dynamic_index_in_dim(pair_rows, head_index // group_size, 1, keepdims=False)
        key_head = pair_head[:, 0].astype(jnp.float32)
        value_head = pair_head[:, 1].astype(jnp.float32)
        scores = jnp.dot(query_head.astype(jnp.float32), key_head.T, precision=lax.Precision.HIGHEST) * score_scale
        scores = jnp.where(causal, scores, -jnp.inf)
        weights = jnp.exp(scores - lax.optimization_barrier(jnp.max(scores, axis=1, keepdims=True)))
        total_weight = lax.optimization_barrier(jnp.sum(weights, axis=1, keepdims=True))
        rounded = lax.optimization_barrier(weights.astype(jnp.bfloat16)).astype(jnp.float32)
        return jnp.dot(rounded, value_head, precision=lax.Precision.HIGHEST) / total_weight
    per_head = lax.map(one_head, (jnp.arange(H, dtype=jnp.int32), jnp.transpose(query_rows, (1, 0, 2))))
    attention = jnp.transpose(per_head, (1, 0, 2)).reshape(KEPT, H * HD)
    update = (router_rows[:, None] * attention).astype(jnp.bfloat16)
    update = lax.optimization_barrier(update).astype(jnp.float32)
    token_rows = (owner_block * TOK_DEV + kept_local[owner_block, slot_index]).astype(jnp.int32)
    return residual.astype(jnp.float32).at[token_rows].add(update).astype(jnp.bfloat16)
```

```python
import math

import jax
import jax.numpy as jnp
from jax import lax
from jax.experimental import pallas as pl
from jax.experimental.pallas import tpu as pltpu
from jax.sharding import Mesh, PartitionSpec as P

H = 64
KVH = 8
HD = 128
TOK_DEV = 1024
CAP = 256
N_CTX = 16
HEADS = 4
ROWS = HEADS * CAP
HALF = 128
GRAN = 16
TILE = 256
CTX = ("y", "xl", "co")
TP = ("z", "xh")
BF = jnp.bfloat16
F32 = jnp.float32
EXP2_SCALE = math.log2(math.e) / math.sqrt(HD)
CONTRACT_LAST = (((1,), (1,)), ((), ()))


def shift(block, axis, distance):
    size = lax.axis_size(axis)
    return lax.ppermute(block, axis, [(i, (i + distance) % size) for i in range(size)])


def shift_x(block, distance):
    def at(x):
        return (x % 2) * 2 + x // 2

    return lax.ppermute(block, ("xl", "xh"), [(at(x), at((x + distance) % 4)) for x in range(4)])


def compact(pieces, rows, live_ref, offset_ref, fill_key, k_buf, v_buf):
    ones = jnp.ones((rows, HD), BF)
    row_in = lax.broadcasted_iota(jnp.int32, (GRAN, 2 * HD), 0)
    for at, (piece, first) in enumerate(pieces):
        live = live_ref[at]
        start = pl.multiple_of(offset_ref[at], GRAN)

        @pl.when(live > 0)
        def _():
            k_buf[pl.ds(start, rows), :] = piece[first : first + rows, :HD]
            v_buf[pl.ds(start, rows), :HD] = piece[first : first + rows, HD:]
            v_buf[pl.ds(start, rows), HD:] = ones

        @pl.when(live % GRAN > 0)
        def _():
            edge = pl.multiple_of(start + (live // GRAN) * GRAN, GRAN)
            inside = row_in < live % GRAN
            keys = k_buf[pl.ds(edge, GRAN), :].astype(F32)
            values = v_buf[pl.ds(edge, GRAN), :].astype(F32)
            fill = jnp.broadcast_to(fill_key.astype(F32), (GRAN, HD))
            k_buf[pl.ds(edge, GRAN), :] = jnp.where(inside[:, :HD], keys, fill).astype(BF)
            v_buf[pl.ds(edge, GRAN), :] = jnp.where(inside, values, 0.0).astype(BF)

    end = pl.multiple_of(offset_ref[len(pieces)], GRAN)
    k_buf[pl.ds(end, TILE), :] = jnp.broadcast_to(fill_key, (TILE, HD))
    v_buf[pl.ds(end, TILE), :] = jnp.zeros((TILE, 2 * HD), BF)
    return (end + TILE - 1) // TILE


def lane_max(scores):
    return jnp.maximum(scores[:, :HD], scores[:, HD:])


def twice(column):
    return jnp.concatenate([column, column], axis=1)


def score_tiles(tiles, q_all, k_buf, s_buf, top_buf):
    def one_tile(tile, _):
        first = pl.multiple_of(tile * TILE, TILE)
        scores = lax.dot_general(
            q_all[...], k_buf[pl.ds(first, TILE), :], CONTRACT_LAST, preferred_element_type=F32
        )
        s_buf[tile] = scores
        top_buf[...] = jnp.maximum(top_buf[...], lane_max(scores))
        return 0

    lax.fori_loop(0, tiles, one_tile, 0)


def weigh_tiles(tiles, top, v_buf, s_buf, sum_ref):
    def one_tile(tile, _):
        first = pl.multiple_of(tile * TILE, TILE)
        weights = jnp.exp2(s_buf[tile] * EXP2_SCALE - twice(top)).astype(BF)
        sum_ref[...] += jnp.dot(weights, v_buf[pl.ds(first, TILE), :], preferred_element_type=F32)
        return 0

    lax.fori_loop(0, tiles, one_tile, 0)


def heads_below(q_ref, q_all):
    for head in range(HEADS):
        q_all[head * CAP : (head + 1) * CAP, :] = q_ref[:, head * HD : (head + 1) * HD]


def near_kernel(live_ref, offset_ref, q_ref, col_ref, other_ref, kept_ref, top_ref, sum_ref, chosen_ref, q_all, k_buf, v_buf, s_buf, near_buf):
    heads_below(q_ref, q_all)
    fill_key = col_ref[0:1, :HD]
    pieces = [(col_ref, CAP * i) for i in (1, 2, 3)] + [(other_ref, CAP * i) for i in range(4)]
    tiles = compact(pieces, CAP, live_ref, offset_ref, fill_key, k_buf, v_buf)
    scores = lax.dot_general(q_all[...], col_ref[:CAP, :HD], CONTRACT_LAST, preferred_element_type=F32)
    rows = lax.broadcasted_iota(jnp.int32, (ROWS, CAP), 0) % CAP
    cols = lax.broadcasted_iota(jnp.int32, (ROWS, CAP), 1)
    scores = jnp.where(cols <= rows, scores, -1e30)
    near_buf[...] = scores
    top_ref[...] = lane_max(scores)
    score_tiles(tiles, q_all, k_buf, s_buf, top_ref)
    top = jnp.broadcast_to(jnp.max(top_ref[...], axis=1, keepdims=True), (ROWS, HD))
    top_ref[...] = top
    top = top * EXP2_SCALE
    weights = jnp.exp2(near_buf[...] * EXP2_SCALE - twice(top)).astype(BF)
    values = jnp.concatenate([col_ref[:CAP, HD:], jnp.ones((CAP, HD), BF)], axis=1)
    sum_ref[...] = jnp.dot(weights, values, preferred_element_type=F32)
    weigh_tiles(tiles, top, v_buf, s_buf, sum_ref)
    place = lax.broadcasted_iota(jnp.int32, (TOK_DEV, CAP), 0)
    chosen_ref[...] = jnp.where(place == kept_ref[...], 1.0, 0.0).astype(BF)


def far_kernel(live_ref, offset_ref, q_ref, col_ref, a_ref, b_ref, oa_ref, ob_ref, top1_ref, sum1_ref, chosen_ref, router_ref, residual_ref, out_ref, q_all, k_buf, v_buf, s_buf, top_buf, sum_buf, out_buf, sems):
    heads_below(q_ref, q_all)
    fill_key = col_ref[0:1, :HD]
    pieces = [(ref, HALF * i) for ref in (a_ref, b_ref, oa_ref, ob_ref) for i in range(4)]
    tiles = compact(pieces, HALF, live_ref, offset_ref, fill_key, k_buf, v_buf)
    top_buf[...] = top1_ref[...]
    score_tiles(tiles, q_all, k_buf, s_buf, top_buf)
    top = jnp.broadcast_to(jnp.max(top_buf[...], axis=1, keepdims=True), (ROWS, HD))
    factor = jnp.exp2((top1_ref[...] - top) * EXP2_SCALE)
    sum_buf[...] = sum1_ref[...] * twice(factor)
    weigh_tiles(tiles, top * EXP2_SCALE, v_buf, s_buf, sum_buf)
    updates = []
    for head in range(HEADS):
        now = slice(head * CAP, (head + 1) * CAP)
        attention = sum_buf[now, :HD] / sum_buf[now, HD:]
        updates.append((router_ref[...] * attention).astype(BF))
    update = jnp.concatenate(updates, axis=1)
    copies = []
    for part, row in enumerate(range(0, TOK_DEV, CAP)):
        now = slice(row, row + CAP)
        added = jnp.dot(chosen_ref[now, :], update, preferred_element_type=F32)
        out_buf[now, :] = (residual_ref[now, :].astype(F32) + added).astype(BF)
        copy = pltpu.make_async_copy(out_buf.at[now], out_ref.at[now], sems.at[part])
        copy.start()
        copies.append(copy)
    for copy in copies:
        copy.wait()


VMEM = pl.BlockSpec(memory_space=pltpu.VMEM)
SMEM = pl.BlockSpec(memory_space=pltpu.SMEM)


def near_part(live, offset, query_rows, col, other, own_kept):
    reach = 7 * CAP
    return pl.pallas_call(
        near_kernel,
        out_shape=[
            jax.ShapeDtypeStruct((ROWS, HD), F32),
            jax.ShapeDtypeStruct((ROWS, 2 * HD), F32),
            jax.ShapeDtypeStruct((TOK_DEV, CAP), BF),
        ],
        in_specs=[SMEM, SMEM] + [VMEM] * 4,
        out_specs=[VMEM] * 3,
        scratch_shapes=[
            pltpu.VMEM((ROWS, HD), BF),
            pltpu.VMEM((reach + TILE, HD), BF),
            pltpu.VMEM((reach + TILE, 2 * HD), BF),
            pltpu.VMEM((reach // TILE, ROWS, TILE), F32),
            pltpu.VMEM((ROWS, CAP), F32),
        ],
        cost_estimate=pl.CostEstimate(flops=2_000_000_000, bytes_accessed=4_000_000, transcendentals=1_500_000),
        compiler_params=pltpu.CompilerParams(vmem_limit_bytes=20 * 1024 * 1024),
    )(live, offset, query_rows, col, other, own_kept)


def far_part(live, offset, query_rows, col, gathered, near, router, residual):
    reach = 8 * CAP
    return pl.pallas_call(
        far_kernel,
        out_shape=jax.ShapeDtypeStruct((TOK_DEV, HEADS * HD), BF),
        in_specs=[SMEM, SMEM] + [VMEM] * 11,
        out_specs=pl.BlockSpec(memory_space=pl.ANY),
        scratch_shapes=[
            pltpu.VMEM((ROWS, HD), BF),
            pltpu.VMEM((reach + TILE, HD), BF),
            pltpu.VMEM((reach + TILE, 2 * HD), BF),
            pltpu.VMEM((reach // TILE, ROWS, TILE), F32),
            pltpu.VMEM((ROWS, HD), F32),
            pltpu.VMEM((ROWS, 2 * HD), F32),
            pltpu.VMEM((TOK_DEV, HEADS * HD), BF),
            pltpu.SemaphoreType.DMA((4,)),
        ],
        compiler_params=pltpu.CompilerParams(vmem_limit_bytes=24 * 1024 * 1024),
    )(live, offset, query_rows, col, *gathered, *near, router, residual)


def live_rows(counts, block, own, first, rows):
    block_count = jnp.sum(jnp.where(block[:, None] == jnp.arange(N_CTX), counts[None, :], 0), axis=1)
    live = jnp.where(block < own, jnp.clip(block_count - first, 0, rows), 0)
    taken = (live + GRAN - 1) // GRAN * GRAN
    size = block.shape[0]
    before = jnp.arange(size + 1)[:, None] > jnp.arange(size)[None, :]
    return live, jnp.sum(jnp.where(before, taken[None, :], 0), axis=1).astype(jnp.int32)


def shards(residual, queries, keys_values, kept_local, router_weight):
    y, xl, co = (lax.axis_index(a) for a in CTX)
    own = (y * 2 + xl) * 2 + co
    rows_tp = queries.shape[1]
    pairs = keys_values.reshape(rows_tp, KVH, 1, 2 * HD)
    pairs = jnp.broadcast_to(pairs, (rows_tp, KVH, 2, 2 * HD)).reshape(rows_tp, 2 * KVH, 2 * HD)
    pairs = lax.all_to_all(pairs, TP, split_axis=1, concat_axis=0, tiled=True)
    pairs = pairs.reshape(CAP, 2 * HD)
    query_rows = queries.reshape(rows_tp, 2 * KVH, HEADS * HD)
    query_rows = lax.all_to_all(query_rows, TP, split_axis=1, concat_axis=0, tiled=True)
    query_rows = query_rows.reshape(CAP, HEADS * HD)

    behind_2, behind_1, behind_3 = (shift(pairs, "y", d) for d in (2, 1, 3))
    col = jnp.concatenate([pairs, behind_1, behind_3, behind_2], axis=0)
    halves = col.reshape(4, 2, HALF, 2 * HD)
    lower = shift_x(halves[:, 0].reshape(4 * HALF, 2 * HD), 1)
    upper = shift_x(halves[:, 1].reshape(4 * HALF, 2 * HD), 3)
    other = shift(col, "co", 1)
    gathered = [lower, upper, shift(lower, "co", 1), shift(upper, "co", 1)]

    counts = jnp.sum((kept_local < TOK_DEV).astype(jnp.int32), axis=1)
    y_of = [(y - d) % 4 for d in (0, 1, 3, 2)]

    def block_of(row, x, core):
        return (row * 2 + x) * 2 + core

    near_block = jnp.stack([block_of(r, xl, co) for r in y_of[1:]] + [block_of(r, xl, 1 - co) for r in y_of])
    near_live, near_offset = live_rows(counts, near_block, own, 0, CAP)
    far_block = jnp.stack([block_of(r, 1 - xl, c) for c in (co, 1 - co) for _ in (0, 1) for r in y_of])
    far_first = jnp.array(([0] * 4 + [HALF] * 4) * 2, jnp.int32)
    far_live, far_offset = live_rows(counts, far_block, own, far_first, HALF)

    own_kept = lax.dynamic_slice_in_dim(kept_local, own, 1, axis=0)
    router = jnp.broadcast_to(router_weight[0].astype(F32)[:, None], (CAP, HD))
    near = near_part(near_live, near_offset, query_rows, col, other, own_kept)
    return far_part(far_live, far_offset, query_rows, col, gathered, near, router, residual)


def solution(mesh):
    grid = Mesh(mesh.devices.reshape(4, 2, 2, 8, 2), CTX + TP)
    placed = (P(CTX, TP), P(CTX, TP, None), P(CTX, TP, None), P(), P(CTX, None))
    return jax.shard_map(shards, mesh=grid, in_specs=placed, out_specs=P(CTX, TP), check_vma=False)
```

```python
import math

import jax
import jax.numpy as jnp
from jax import lax
from jax.experimental import pallas as pl
from jax.experimental.pallas import tpu as pltpu
from jax.sharding import Mesh, PartitionSpec as P

H = 64
KVH = 8
HD = 128
TOK_DEV = 1024
CAP = 256
N_CTX = 16
HEADS = 4
ROWS = HEADS * CAP
HALF = 128
GRAN = 16
TILE = 256
PIECES = 8
PIECES_ALL = 4 * PIECES
FIRST = (0, PIECES, 3 * PIECES, 4 * PIECES)
CTX = ("y", "xl", "co")
TP = ("z", "xh")
BF = jnp.bfloat16
F32 = jnp.float32
HIDDEN = -1e30
EXP2_SCALE = math.log2(math.e) / math.sqrt(HD)
CONTRACT_LAST = (((1,), (1,)), ((), ()))
VMEM = pl.BlockSpec(memory_space=pltpu.VMEM)
SMEM = pl.BlockSpec(memory_space=pltpu.SMEM)
ANY = pl.BlockSpec(memory_space=pltpu.HBM)
STATE = [jax.ShapeDtypeStruct((ROWS, HD), F32), jax.ShapeDtypeStruct((ROWS, 2 * HD), F32)]


def buffers(pieces):
    rows = pieces * HALF + TILE
    return [pltpu.VMEM((rows, HD), BF), pltpu.VMEM((rows, 2 * HD), BF)]


def shift(block, axis, distance):
    size = lax.axis_size(axis)
    return lax.ppermute(block, axis, [(i, (i + distance) % size) for i in range(size)])


def shift_x(block, distance):
    def at(x):
        return (x % 2) * 2 + x // 2

    return lax.ppermute(block, ("xl", "xh"), [(at(x), at((x + distance) % 4)) for x in range(4)])


def compact(pieces, group, table_ref, fill_ref, k_buf, v_buf):
    row_in = lax.broadcasted_iota(jnp.int32, (HALF, HD), 0)
    fill = jnp.broadcast_to(fill_ref[0:1, :HD], (HALF, HD))
    for at, (piece, first) in enumerate(pieces):
        start = pl.multiple_of(table_ref[PIECES_ALL + FIRST[group] + at], GRAN)
        inside = row_in < table_ref[FIRST[group] + at]
        rows, now = pl.ds(start, HALF), slice(first, first + HALF)
        k_buf[rows, :] = jnp.where(inside, piece[now, :HD], fill)
        v_buf[rows, :HD] = jnp.where(inside, piece[now, HD:], jnp.zeros((HALF, HD), BF))
        v_buf[rows, HD:] = jnp.where(inside, 1.0, 0.0).astype(BF)
    end = pl.multiple_of(table_ref[2 * PIECES_ALL + group], GRAN)
    k_buf[pl.ds(end, TILE), :] = jnp.broadcast_to(fill_ref[0:1, :HD], (TILE, HD))
    v_buf[pl.ds(end, TILE), :] = jnp.zeros((TILE, 2 * HD), BF)
    return (end + TILE - 1) // TILE


def twice(column):
    return jnp.concatenate([column, column], axis=1)


def soften(scores, before):
    top = before
    for lane in range(0, scores.shape[1], HD):
        now = scores[:, lane : lane + HD]
        top = now if top is None else jnp.maximum(top, now)
    top = jnp.broadcast_to(jnp.max(top, axis=1, keepdims=True), (CAP, HD))
    shifted = top * EXP2_SCALE
    shifted = jnp.concatenate([shifted] * (scores.shape[1] // HD), axis=1)
    return top, jnp.exp2(scores * EXP2_SCALE - shifted).astype(BF)


def absorb(tiles, q_ref, k_buf, v_buf, old, new):
    (top_old, sum_old), (top_new, sum_new) = old, new
    for count in range((k_buf.shape[0] - TILE) // TILE + 1):

        @pl.when(tiles == count)
        def _():
            if count == 0:
                top_new[...] = top_old[...]
                sum_new[...] = sum_old[...]
                return
            keys = count * TILE
            for head in range(HEADS):
                now = slice(head * CAP, (head + 1) * CAP)
                query = q_ref[:, head * HD : (head + 1) * HD]
                scores = lax.dot_general(
                    query, k_buf[:keys, :], CONTRACT_LAST, preferred_element_type=F32
                )
                before = top_old[now, :]
                top, weights = soften(scores, before)
                factor = jnp.exp2((before - top) * EXP2_SCALE)
                added = jnp.dot(weights, v_buf[:keys, :], preferred_element_type=F32)
                sum_new[now, :] = sum_old[now, :] * twice(factor) + added
                top_new[now, :] = top


def pieces_of(*refs):
    return [(ref, HALF * i) for ref in refs for i in range(PIECES // 2)]


def own_kernel(table_ref, q_ref, lower_ref, upper_ref, top_ref, sum_ref, k_buf, v_buf):
    rows = lax.broadcasted_iota(jnp.int32, (CAP, CAP), 0)
    cols = lax.broadcasted_iota(jnp.int32, (CAP, CAP), 1)
    tiles = compact(pieces_of(lower_ref, upper_ref), 0, table_ref, lower_ref, k_buf, v_buf)
    keys = lower_ref[:CAP, :HD]
    values = jnp.concatenate([lower_ref[:CAP, HD:], jnp.ones((CAP, HD), BF)], axis=1)
    for head in range(HEADS):
        now = slice(head * CAP, (head + 1) * CAP)
        query = q_ref[:, head * HD : (head + 1) * HD]
        scores = lax.dot_general(query, keys, CONTRACT_LAST, preferred_element_type=F32)
        top, weights = soften(jnp.where(cols <= rows, scores, HIDDEN), None)
        top_ref[now, :] = top
        sum_ref[now, :] = jnp.dot(weights, values, preferred_element_type=F32)
    state = (top_ref, sum_ref)
    absorb(tiles, q_ref, k_buf, v_buf, state, state)


def more_kernel(table_ref, q_ref, fill_ref, *rest):
    blocks, state, (top_ref, sum_ref, k_buf, v_buf) = rest[:-6], rest[-6:-4], rest[-4:]
    tiles = compact(pieces_of(*blocks), 1, table_ref, fill_ref, k_buf, v_buf)
    absorb(tiles, q_ref, k_buf, v_buf, state, (top_ref, sum_ref))


def last_kernel(table_ref, q_ref, fill_ref, lower_ref, upper_ref, top0, sum0, kept_ref, router_ref, residual_ref, out_ref, k_buf, v_buf, top_ref, sum_ref, residual_buf, out_buf, sems):
    fetch = pltpu.make_async_copy(residual_ref, residual_buf, sems.at[4])
    fetch.start()
    pieces = pieces_of(lower_ref, upper_ref)
    tiles = compact(pieces, 2, table_ref, fill_ref, k_buf, v_buf)
    absorb(tiles, q_ref, k_buf, v_buf, (top0, sum0), (top_ref, sum_ref))
    updates = []
    for head in range(HEADS):
        now = slice(head * CAP, (head + 1) * CAP)
        attention = sum_ref[now, :HD] / sum_ref[now, HD:]
        updates.append((router_ref[...] * attention).astype(BF))
    update = jnp.concatenate(updates, axis=1)
    kept = kept_ref[pl.ds(table_ref[2 * PIECES_ALL + 3], 1), :]
    fetch.wait()
    copies = []
    for part, row in enumerate(range(0, TOK_DEV, CAP)):
        now = slice(row, row + CAP)
        place = lax.broadcasted_iota(jnp.int32, (CAP, CAP), 0) + row
        chosen = jnp.where(place == kept, 1.0, 0.0).astype(BF)
        added = jnp.dot(chosen, update, preferred_element_type=F32)
        out_buf[now, :] = (residual_buf[now, :].astype(F32) + added).astype(BF)
        copy = pltpu.make_async_copy(out_buf.at[now], out_ref.at[now], sems.at[part])
        copy.start()
        copies.append(copy)
    for copy in copies:
        copy.wait()


def params(mebibytes):
    return pltpu.CompilerParams(vmem_limit_bytes=mebibytes * 1024 * 1024)


SMALL = pl.CostEstimate(flops=1_000_000, bytes_accessed=10_000, transcendentals=1_000)


def sorted_kernel(queries_ref, pairs_ref, out_ref, buf, in_sems, out_sems):
    width = HEADS * HD
    arrive, leave = [], []
    for to in range(2 * KVH):
        here = queries_ref.at[0, :, pl.ds(to * width, width)]
        arrive.append(pltpu.make_async_copy(here, buf.at[to, :, pl.ds(0, width)], in_sems.at[2 * to]))
        here = pairs_ref.at[0, :, pl.ds(to // 2 * 2 * HD, 2 * HD)]
        arrive.append(pltpu.make_async_copy(here, buf.at[to, :, pl.ds(width, 2 * HD)], in_sems.at[2 * to + 1]))
        leave.append(pltpu.make_async_copy(buf.at[to], out_ref.at[to], out_sems.at[to]))
    for copy in arrive:
        copy.start()
    for to in range(2 * KVH):
        arrive[2 * to].wait()
        arrive[2 * to + 1].wait()
        leave[to].start()
    for copy in leave:
        copy.wait()


def sorted_part(queries, pairs):
    shape = (2 * KVH, queries.shape[1], (HEADS + 2) * HD)
    return pl.pallas_call(
        sorted_kernel,
        out_shape=jax.ShapeDtypeStruct(shape, BF),
        in_specs=[ANY, ANY],
        out_specs=ANY,
        scratch_shapes=[
            pltpu.VMEM(shape, BF),
            pltpu.SemaphoreType.DMA((4 * KVH,)),
            pltpu.SemaphoreType.DMA((2 * KVH,)),
        ],
        compiler_params=params(60),
    )(queries, pairs)


def own_part(table, query_rows, lower, upper):
    return pl.pallas_call(
        own_kernel,
        out_shape=STATE,
        in_specs=[SMEM] + [VMEM] * 3,
        out_specs=[VMEM] * 2,
        scratch_shapes=buffers(PIECES),
        cost_estimate=SMALL,
        compiler_params=params(16),
    )(table, query_rows, lower, upper)


def more_part(table, query_rows, fill, blocks, state):
    return pl.pallas_call(
        more_kernel,
        out_shape=STATE,
        in_specs=[SMEM] + [VMEM] * (4 + len(blocks)),
        out_specs=[VMEM] * 2,
        scratch_shapes=buffers(2 * PIECES),
        cost_estimate=SMALL,
        compiler_params=params(16),
    )(table, query_rows, fill, *blocks, *state)


def last_part(table, query_rows, fill, blocks, state, kept_local, router, residual):
    return pl.pallas_call(
        last_kernel,
        out_shape=jax.ShapeDtypeStruct((TOK_DEV, HEADS * HD), BF),
        in_specs=[SMEM] + [VMEM] * 8 + [ANY],
        out_specs=ANY,
        scratch_shapes=buffers(PIECES)
        + [pltpu.VMEM(s.shape, s.dtype) for s in STATE]
        + [pltpu.VMEM((TOK_DEV, HEADS * HD), BF)] * 2
        + [pltpu.SemaphoreType.DMA((5,))],
        compiler_params=params(16),
    )(table, query_rows, fill, *blocks, *state, kept_local, router, residual)


def tables(kept_local, y, xl, co):
    own = (y * 2 + xl) * 2 + co
    counts = jnp.sum((kept_local < TOK_DEV).astype(jnp.int32), axis=1)
    at = jnp.arange(4 * PIECES, dtype=jnp.int32)
    group, piece = at // PIECES, at % PIECES
    behind, half = piece // 2, piece % 2
    behind = behind ^ (behind // 2)
    block = (((y - behind + 4) % 4) * 2 + (xl ^ (group // 2))) * 2 + (co ^ (group % 2))
    block_count = jnp.sum(jnp.where(block[:, None] == jnp.arange(N_CTX), counts[None, :], 0), axis=1)
    live = jnp.where(block < own, jnp.clip(block_count - half * HALF, 0, HALF), 0)
    taken = (live + GRAN - 1) // GRAN * GRAN
    part = (group + 1) // 2
    to = jnp.arange(PIECES_ALL + 3, dtype=jnp.int32)[:, None]
    to_part = jnp.where(to < PIECES_ALL, (to // PIECES + 1) // 2, to - PIECES_ALL)
    counted = (to_part == part[None, :]) & (at[None, :] < to)
    offset = jnp.sum(jnp.where(counted, taken[None, :], 0), axis=1)
    return jnp.concatenate([live, offset, jnp.broadcast_to(own, (1,))]).astype(jnp.int32)


def shards(residual, queries, keys_values, kept_local, router_weight):
    y, xl, co = (lax.axis_index(a) for a in CTX)
    sent = sorted_part(queries, keys_values)
    sent = lax.all_to_all(sent, TP, split_axis=0, concat_axis=0, tiled=True)
    sent = sent.reshape(CAP, (HEADS + 2) * HD)
    query_rows, pairs = sent[:, : HEADS * HD], sent[:, HEADS * HD :]
    table = tables(kept_local, y, xl, co)
    router = jnp.broadcast_to(router_weight[0].astype(F32)[:, None], (CAP, HD))
    pairs, table, router = lax.optimization_barrier((pairs, table, router))

    behind_1, behind_3, behind_2 = (shift(pairs, "y", d) for d in (1, 3, 2))
    lower = jnp.concatenate([pairs, behind_1], axis=0)
    upper = jnp.concatenate([behind_3, behind_2], axis=0)
    lower_x, upper_x = shift_x(lower, 1), shift_x(upper, 3)
    state = own_part(table, query_rows, lower, upper)
    low, up, *state = lax.optimization_barrier((lower, upper, *state))
    others = [shift(low, "co", 1), shift(up, "co", 1)]
    lower_x, upper_x, *state = lax.optimization_barrier((lower_x, upper_x, *state))
    swapped = [shift(lower_x, "co", 1), shift(upper_x, "co", 1)]
    state = more_part(table, query_rows, pairs, [*others, lower_x, upper_x], state)
    return last_part(table, query_rows, pairs, swapped, state, kept_local, router, residual)


def solution(mesh):
    grid = Mesh(mesh.devices.reshape(4, 2, 2, 8, 2), CTX + TP)
    placed = (P(CTX, TP), P(CTX, TP, None), P(CTX, TP, None), P(), P(CTX, None))
    return jax.shard_map(shards, mesh=grid, in_specs=placed, out_specs=P(CTX, TP), check_vma=False)
```

```python
import math

import jax
import jax.numpy as jnp
from jax import lax
from jax.experimental import pallas as pl
from jax.experimental.pallas import tpu as pltpu
from jax.sharding import Mesh, PartitionSpec as P

H = 64
KVH = 8
HD = 128
TOK_DEV = 1024
CAP = 256
N_CTX = 16
HEADS = 4
ROWS = HEADS * CAP
HALF = 128
GRAN = 16
TILE = 256
PIECES = 8
PIECES_ALL = 4 * PIECES
FIRST = (0, PIECES, 3 * PIECES, 4 * PIECES)
CTX = ("y", "xl", "co")
TP = ("z", "xh")
BF = jnp.bfloat16
F32 = jnp.float32
HIDDEN = -1e30
EXP2_SCALE = math.log2(math.e) / math.sqrt(HD)
CONTRACT_LAST = (((1,), (1,)), ((), ()))
VMEM = pl.BlockSpec(memory_space=pltpu.VMEM)
SMEM = pl.BlockSpec(memory_space=pltpu.SMEM)
ANY = pl.BlockSpec(memory_space=pltpu.HBM)
STATE = [jax.ShapeDtypeStruct((ROWS, HD), F32), jax.ShapeDtypeStruct((ROWS, 2 * HD), F32)]


def buffers(pieces):
    rows = pieces * HALF + TILE
    return [pltpu.VMEM((rows, HD), BF), pltpu.VMEM((rows, 2 * HD), BF)]


def shift(block, axis, distance):
    size = lax.axis_size(axis)
    return lax.ppermute(block, axis, [(i, (i + distance) % size) for i in range(size)])


def shift_x(block, distance):
    def at(x):
        return (x % 2) * 2 + x // 2

    return lax.ppermute(block, ("xl", "xh"), [(at(x), at((x + distance) % 4)) for x in range(4)])


def compact(pieces, group, table_ref, fill_ref, k_buf, v_buf):
    row_in = lax.broadcasted_iota(jnp.int32, (HALF, HD), 0)
    fill = jnp.broadcast_to(fill_ref[0:1, :HD], (HALF, HD))
    for at, (piece, first) in enumerate(pieces):
        start = pl.multiple_of(table_ref[PIECES_ALL + FIRST[group] + at], GRAN)
        inside = row_in < table_ref[FIRST[group] + at]
        rows, now = pl.ds(start, HALF), slice(first, first + HALF)
        k_buf[rows, :] = jnp.where(inside, piece[now, :HD], fill)
        v_buf[rows, :HD] = jnp.where(inside, piece[now, HD:], jnp.zeros((HALF, HD), BF))
        v_buf[rows, HD:] = jnp.where(inside, 1.0, 0.0).astype(BF)
    end = pl.multiple_of(table_ref[2 * PIECES_ALL + group], GRAN)
    k_buf[pl.ds(end, TILE), :] = jnp.broadcast_to(fill_ref[0:1, :HD], (TILE, HD))
    v_buf[pl.ds(end, TILE), :] = jnp.zeros((TILE, 2 * HD), BF)
    return (end + TILE - 1) // TILE


def twice(column):
    return jnp.concatenate([column, column], axis=1)


def soften(scores, before):
    top = before
    for lane in range(0, scores.shape[1], HD):
        now = scores[:, lane : lane + HD]
        top = now if top is None else jnp.maximum(top, now)
    top = jnp.broadcast_to(jnp.max(top, axis=1, keepdims=True), (CAP, HD))
    shifted = top * EXP2_SCALE
    shifted = jnp.concatenate([shifted] * (scores.shape[1] // HD), axis=1)
    return top, jnp.exp2(scores * EXP2_SCALE - shifted).astype(BF)


def absorb(tiles, q_ref, k_buf, v_buf, old, new):
    (top_old, sum_old), (top_new, sum_new) = old, new
    for count in range((k_buf.shape[0] - TILE) // TILE + 1):

        @pl.when(tiles == count)
        def _():
            if count == 0:
                top_new[...] = top_old[...]
                sum_new[...] = sum_old[...]
                return
            keys = count * TILE
            for head in range(HEADS):
                now = slice(head * CAP, (head + 1) * CAP)
                query = q_ref[:, head * HD : (head + 1) * HD]
                scores = lax.dot_general(
                    query, k_buf[:keys, :], CONTRACT_LAST, preferred_element_type=F32
                )
                before = top_old[now, :]
                top, weights = soften(scores, before)
                factor = jnp.exp2((before - top) * EXP2_SCALE)
                added = jnp.dot(weights, v_buf[:keys, :], preferred_element_type=F32)
                sum_new[now, :] = sum_old[now, :] * twice(factor) + added
                top_new[now, :] = top


def pieces_of(*refs):
    return [(ref, row) for ref in refs for row in range(0, ref.shape[0], HALF)]


def own_kernel(table_ref, q_ref, lower_ref, upper_ref, top_ref, sum_ref, k_buf, v_buf):
    rows = lax.broadcasted_iota(jnp.int32, (CAP, CAP), 0)
    cols = lax.broadcasted_iota(jnp.int32, (CAP, CAP), 1)
    tiles = compact(pieces_of(lower_ref, upper_ref), 0, table_ref, lower_ref, k_buf, v_buf)
    keys = lower_ref[:CAP, :HD]
    values = jnp.concatenate([lower_ref[:CAP, HD:], jnp.ones((CAP, HD), BF)], axis=1)
    for head in range(HEADS):
        now = slice(head * CAP, (head + 1) * CAP)
        query = q_ref[:, head * HD : (head + 1) * HD]
        scores = lax.dot_general(query, keys, CONTRACT_LAST, preferred_element_type=F32)
        top, weights = soften(jnp.where(cols <= rows, scores, HIDDEN), None)
        top_ref[now, :] = top
        sum_ref[now, :] = jnp.dot(weights, values, preferred_element_type=F32)
    state = (top_ref, sum_ref)
    absorb(tiles, q_ref, k_buf, v_buf, state, state)


def more_kernel(table_ref, q_ref, fill_ref, *rest):
    blocks, state, (top_ref, sum_ref, k_buf, v_buf) = rest[:-6], rest[-6:-4], rest[-4:]
    tiles = compact(pieces_of(*blocks), 1, table_ref, fill_ref, k_buf, v_buf)
    absorb(tiles, q_ref, k_buf, v_buf, state, (top_ref, sum_ref))


def last_kernel(table_ref, q_ref, fill_ref, own_ref, lower_ref, upper_ref, top0, sum0, kept_ref, router_ref, residual_ref, out_ref, k_buf, v_buf, top_ref, sum_ref, residual_buf, out_buf, sems):
    fetch = pltpu.make_async_copy(residual_ref, residual_buf, sems.at[4])
    fetch.start()
    pieces = pieces_of(own_ref, lower_ref, upper_ref)
    tiles = compact(pieces, 2, table_ref, fill_ref, k_buf, v_buf)
    absorb(tiles, q_ref, k_buf, v_buf, (top0, sum0), (top_ref, sum_ref))
    updates = []
    for head in range(HEADS):
        now = slice(head * CAP, (head + 1) * CAP)
        attention = sum_ref[now, :HD] / sum_ref[now, HD:]
        updates.append((router_ref[...] * attention).astype(BF))
    update = jnp.concatenate(updates, axis=1)
    kept = kept_ref[pl.ds(table_ref[2 * PIECES_ALL + 3], 1), :]
    fetch.wait()
    copies = []
    for part, row in enumerate(range(0, TOK_DEV, CAP)):
        now = slice(row, row + CAP)
        place = lax.broadcasted_iota(jnp.int32, (CAP, CAP), 0) + row
        chosen = jnp.where(place == kept, 1.0, 0.0).astype(BF)
        added = jnp.dot(chosen, update, preferred_element_type=F32)
        out_buf[now, :] = (residual_buf[now, :].astype(F32) + added).astype(BF)
        copy = pltpu.make_async_copy(out_buf.at[now], out_ref.at[now], sems.at[part])
        copy.start()
        copies.append(copy)
    for copy in copies:
        copy.wait()


def params(mebibytes):
    return pltpu.CompilerParams(vmem_limit_bytes=mebibytes * 1024 * 1024)


SMALL = pl.CostEstimate(flops=1_000_000, bytes_accessed=10_000, transcendentals=1_000)


def sorted_kernel(queries_ref, pairs_ref, out_ref, q_buf, kv_buf, out_buf, in_sems, out_sems):
    width, quarter = HEADS * HD, KVH // 2
    arrive = [pltpu.make_async_copy(pairs_ref.at[0], kv_buf, in_sems.at[4])]
    for part in range(4):
        now = pl.ds(part * quarter * width, quarter * width)
        arrive.append(pltpu.make_async_copy(queries_ref.at[0, :, now], q_buf.at[:, now], in_sems.at[part]))
    for copy in arrive:
        copy.start()
    arrive[0].wait()
    leave = []
    for part in range(4):
        arrive[part + 1].wait()
        for to in range(part * quarter, (part + 1) * quarter):
            group = to // 2
            out_buf[to, :, :width] = q_buf[:, to * width : (to + 1) * width]
            out_buf[to, :, width:] = kv_buf[:, group * 2 * HD : (group + 1) * 2 * HD]
        now = pl.ds(part * quarter, quarter)
        leave.append(pltpu.make_async_copy(out_buf.at[now], out_ref.at[now], out_sems.at[part]))
        leave[-1].start()
    for copy in leave:
        copy.wait()


def sorted_part(queries, pairs):
    shape = (2 * KVH, queries.shape[1], (HEADS + 2) * HD)
    return pl.pallas_call(
        sorted_kernel,
        out_shape=jax.ShapeDtypeStruct(shape, BF),
        in_specs=[ANY, ANY],
        out_specs=ANY,
        scratch_shapes=[
            pltpu.VMEM(queries.shape[1:], BF),
            pltpu.VMEM(pairs.shape[1:], BF),
            pltpu.VMEM(shape, BF),
            pltpu.SemaphoreType.DMA((5,)),
            pltpu.SemaphoreType.DMA((4,)),
        ],
        compiler_params=params(60),
    )(queries, pairs)


def own_part(table, query_rows, lower, upper):
    return pl.pallas_call(
        own_kernel,
        out_shape=STATE,
        in_specs=[SMEM] + [VMEM] * 3,
        out_specs=[VMEM] * 2,
        scratch_shapes=buffers(PIECES),
        cost_estimate=SMALL,
        compiler_params=params(16),
    )(table, query_rows, lower, upper)


def more_part(table, query_rows, fill, blocks, state):
    return pl.pallas_call(
        more_kernel,
        out_shape=STATE,
        in_specs=[SMEM] + [VMEM] * (4 + len(blocks)),
        out_specs=[VMEM] * 2,
        scratch_shapes=buffers(2 * PIECES),
        cost_estimate=SMALL,
        compiler_params=params(16),
    )(table, query_rows, fill, *blocks, *state)


def last_part(table, query_rows, fill, blocks, state, kept_local, router, residual):
    return pl.pallas_call(
        last_kernel,
        out_shape=jax.ShapeDtypeStruct((TOK_DEV, HEADS * HD), BF),
        in_specs=[SMEM] + [VMEM] * 9 + [ANY],
        out_specs=ANY,
        scratch_shapes=buffers(PIECES)
        + [pltpu.VMEM(s.shape, s.dtype) for s in STATE]
        + [pltpu.VMEM((TOK_DEV, HEADS * HD), BF)] * 2
        + [pltpu.SemaphoreType.DMA((5,))],
        compiler_params=params(16),
    )(table, query_rows, fill, *blocks, *state, kept_local, router, residual)


def tables(kept_local, y, xl, co):
    own = (y * 2 + xl) * 2 + co
    counts = jnp.sum((kept_local < TOK_DEV).astype(jnp.int32), axis=1)
    at = jnp.arange(4 * PIECES, dtype=jnp.int32)
    group, piece = at // PIECES, at % PIECES
    straight = (piece // 2) ^ (piece // 4)
    split = jnp.where(piece < 4, piece // 2, jnp.where((piece == 4) | (piece == 7), 2, 3))
    behind = jnp.where(group < 2, straight, split)
    half = jnp.where((group < 2) | (piece < 4), piece % 2, jnp.where(piece == 5, 0, piece // 6))
    block = (((y - behind + 4) % 4) * 2 + (xl ^ (group // 2))) * 2 + (co ^ (group % 2))
    block_count = jnp.sum(jnp.where(block[:, None] == jnp.arange(N_CTX), counts[None, :], 0), axis=1)
    live = jnp.where(block < own, jnp.clip(block_count - half * HALF, 0, HALF), 0)
    taken = (live + GRAN - 1) // GRAN * GRAN
    part = (group + 1) // 2
    to = jnp.arange(PIECES_ALL + 3, dtype=jnp.int32)[:, None]
    to_part = jnp.where(to < PIECES_ALL, (to // PIECES + 1) // 2, to - PIECES_ALL)
    counted = (to_part == part[None, :]) & (at[None, :] < to)
    offset = jnp.sum(jnp.where(counted, taken[None, :], 0), axis=1)
    return jnp.concatenate([live, offset, jnp.broadcast_to(own, (1,))]).astype(jnp.int32)


def shards(residual, queries, keys_values, kept_local, router_weight):
    y, xl, co = (lax.axis_index(a) for a in CTX)
    sent = sorted_part(queries, keys_values)
    sent = lax.all_to_all(sent, TP, split_axis=0, concat_axis=0, tiled=True)
    sent = sent.reshape(CAP, (HEADS + 2) * HD)
    query_rows, pairs = sent[:, : HEADS * HD], sent[:, HEADS * HD :]
    table = tables(kept_local, y, xl, co)
    router = jnp.broadcast_to(router_weight[0].astype(F32)[:, None], (CAP, HD))
    pairs, table, router = lax.optimization_barrier((pairs, table, router))

    behind_1, behind_3, behind_2 = (shift(pairs, "y", d) for d in (1, 3, 2))
    own_x = shift_x(pairs, 1)
    lower = jnp.concatenate([pairs, behind_1], axis=0)
    upper = jnp.concatenate([behind_3, behind_2], axis=0)
    lower_x = shift_x(jnp.concatenate([behind_1, behind_2[:HALF]], axis=0), 1)
    upper_x = shift_x(jnp.concatenate([behind_3, behind_2[HALF:]], axis=0), 3)
    state = own_part(table, query_rows, lower, upper)
    low, up, *state = lax.optimization_barrier((lower, upper, *state))
    others = [shift(low, "co", 1), shift(up, "co", 1)]
    own_x, lower_x, upper_x, *state = lax.optimization_barrier((own_x, lower_x, upper_x, *state))
    arrived = [own_x, lower_x, upper_x]
    swapped = [shift(x, "co", 1) for x in arrived]
    state = more_part(table, query_rows, pairs, [*others, *arrived], state)
    return last_part(table, query_rows, pairs, swapped, state, kept_local, router, residual)


def solution(mesh):
    grid = Mesh(mesh.devices.reshape(4, 2, 2, 8, 2), CTX + TP)
    placed = (P(CTX, TP), P(CTX, TP, None), P(CTX, TP, None), P(), P(CTX, None))
    return jax.shard_map(shards, mesh=grid, in_specs=placed, out_specs=P(CTX, TP), check_vma=False)
```

```python
import math

import jax
import jax.numpy as jnp
from jax import lax
from jax.experimental import pallas as pl
from jax.experimental.pallas import tpu as pltpu
from jax.sharding import Mesh, PartitionSpec as P

H = 64
KVH = 8
HD = 128
TOK_DEV = 1024
CAP = 256
N_CTX = 16
HEADS = 4
ROWS = HEADS * CAP
HALF = 128
GRAN = 16
TILE = 256
PIECES = 8
PIECES_ALL = 4 * PIECES
FIRST = (0, PIECES, 3 * PIECES, 4 * PIECES)
CTX = ("y", "xl", "co")
TP = ("z", "xh")
BF = jnp.bfloat16
F32 = jnp.float32
HIDDEN = -1e30
EXP2_SCALE = math.log2(math.e) / math.sqrt(HD)
CONTRACT_LAST = (((1,), (1,)), ((), ()))
VMEM = pl.BlockSpec(memory_space=pltpu.VMEM)
SMEM = pl.BlockSpec(memory_space=pltpu.SMEM)
ANY = pl.BlockSpec(memory_space=pltpu.HBM)
STATE = [jax.ShapeDtypeStruct((ROWS, HD), F32), jax.ShapeDtypeStruct((ROWS, 2 * HD), F32)]


def buffers(pieces):
    rows = pieces * HALF + TILE
    return [pltpu.VMEM((rows, HD), BF), pltpu.VMEM((rows, 2 * HD), BF)]


def shift(block, axis, distance):
    size = lax.axis_size(axis)
    return lax.ppermute(block, axis, [(i, (i + distance) % size) for i in range(size)])


def shift_x(block, distance):
    def at(x):
        return (x % 2) * 2 + x // 2

    return lax.ppermute(block, ("xl", "xh"), [(at(x), at((x + distance) % 4)) for x in range(4)])


def compact(pieces, group, table_ref, fill_ref, k_buf, v_buf):
    row_in = lax.broadcasted_iota(jnp.int32, (HALF, HD), 0)
    fill = jnp.broadcast_to(fill_ref[0:1, :HD], (HALF, HD))
    for at, (piece, first) in enumerate(pieces):
        start = pl.multiple_of(table_ref[PIECES_ALL + FIRST[group] + at], GRAN)
        live = table_ref[FIRST[group] + at]
        rows, now = pl.ds(start, HALF), slice(first, first + HALF)

        @pl.when(live > 0)
        def _():
            inside = row_in < live
            k_buf[rows, :] = jnp.where(inside, piece[now, :HD], fill)
            v_buf[rows, :HD] = jnp.where(inside, piece[now, HD:], jnp.zeros((HALF, HD), BF))
            v_buf[rows, HD:] = jnp.where(inside, 1.0, 0.0).astype(BF)

    end = pl.multiple_of(table_ref[2 * PIECES_ALL + group], GRAN)
    k_buf[pl.ds(end, TILE), :] = jnp.broadcast_to(fill_ref[0:1, :HD], (TILE, HD))
    v_buf[pl.ds(end, TILE), :] = jnp.zeros((TILE, 2 * HD), BF)
    return (end + TILE - 1) // TILE


def twice(column):
    return jnp.concatenate([column, column], axis=1)


def soften(scores, before):
    top = before
    for lane in range(0, scores.shape[1], HD):
        now = scores[:, lane : lane + HD]
        top = now if top is None else jnp.maximum(top, now)
    top = jnp.broadcast_to(jnp.max(top, axis=1, keepdims=True), (CAP, HD))
    shifted = top * EXP2_SCALE
    shifted = jnp.concatenate([shifted] * (scores.shape[1] // HD), axis=1)
    return top, jnp.exp2(scores * EXP2_SCALE - shifted).astype(BF)


def absorb(tiles, q_ref, k_buf, v_buf, old, new):
    (top_old, sum_old), (top_new, sum_new) = old, new
    for count in range((k_buf.shape[0] - TILE) // TILE + 1):

        @pl.when(tiles == count)
        def _():
            if count == 0:
                top_new[...] = top_old[...]
                sum_new[...] = sum_old[...]
                return
            keys = count * TILE
            for head in range(HEADS):
                now = slice(head * CAP, (head + 1) * CAP)
                query = q_ref[:, head * HD : (head + 1) * HD]
                scores = lax.dot_general(
                    query, k_buf[:keys, :], CONTRACT_LAST, preferred_element_type=F32
                )
                before = top_old[now, :]
                top, weights = soften(scores, before)
                factor = jnp.exp2((before - top) * EXP2_SCALE)
                added = jnp.dot(weights, v_buf[:keys, :], preferred_element_type=F32)
                sum_new[now, :] = sum_old[now, :] * twice(factor) + added
                top_new[now, :] = top


def pieces_of(*refs):
    return [(ref, row) for ref in refs for row in range(0, ref.shape[0], HALF)]


def own_kernel(table_ref, q_ref, lower_ref, upper_ref, top_ref, sum_ref, k_buf, v_buf):
    rows = lax.broadcasted_iota(jnp.int32, (CAP, CAP), 0)
    cols = lax.broadcasted_iota(jnp.int32, (CAP, CAP), 1)
    tiles = compact(pieces_of(lower_ref, upper_ref), 0, table_ref, lower_ref, k_buf, v_buf)
    keys = lower_ref[:CAP, :HD]
    values = jnp.concatenate([lower_ref[:CAP, HD:], jnp.ones((CAP, HD), BF)], axis=1)
    for head in range(HEADS):
        now = slice(head * CAP, (head + 1) * CAP)
        query = q_ref[:, head * HD : (head + 1) * HD]
        scores = lax.dot_general(query, keys, CONTRACT_LAST, preferred_element_type=F32)
        top, weights = soften(jnp.where(cols <= rows, scores, HIDDEN), None)
        top_ref[now, :] = top
        sum_ref[now, :] = jnp.dot(weights, values, preferred_element_type=F32)
    state = (top_ref, sum_ref)
    absorb(tiles, q_ref, k_buf, v_buf, state, state)


def more_kernel(table_ref, q_ref, fill_ref, *rest):
    blocks, state, (top_ref, sum_ref, k_buf, v_buf) = rest[:-6], rest[-6:-4], rest[-4:]
    tiles = compact(pieces_of(*blocks), 1, table_ref, fill_ref, k_buf, v_buf)
    absorb(tiles, q_ref, k_buf, v_buf, state, (top_ref, sum_ref))


def last_kernel(table_ref, q_ref, fill_ref, own_ref, lower_ref, upper_ref, top0, sum0, kept_ref, router_ref, residual_ref, out_ref, k_buf, v_buf, top_ref, sum_ref, residual_buf, out_buf, sems):
    fetch = pltpu.make_async_copy(residual_ref, residual_buf, sems.at[4])
    fetch.start()
    pieces = pieces_of(own_ref, lower_ref, upper_ref)
    tiles = compact(pieces, 2, table_ref, fill_ref, k_buf, v_buf)
    absorb(tiles, q_ref, k_buf, v_buf, (top0, sum0), (top_ref, sum_ref))
    updates = []
    for head in range(HEADS):
        now = slice(head * CAP, (head + 1) * CAP)
        attention = sum_ref[now, :HD] / sum_ref[now, HD:]
        updates.append((router_ref[...] * attention).astype(BF))
    update = jnp.concatenate(updates, axis=1)
    kept = kept_ref[pl.ds(table_ref[2 * PIECES_ALL + 3], 1), :]
    fetch.wait()
    copies = []
    for part, row in enumerate(range(0, TOK_DEV, CAP)):
        now = slice(row, row + CAP)
        place = lax.broadcasted_iota(jnp.int32, (CAP, CAP), 0) + row
        chosen = jnp.where(place == kept, 1.0, 0.0).astype(BF)
        added = jnp.dot(chosen, update, preferred_element_type=F32)
        out_buf[now, :] = (residual_buf[now, :].astype(F32) + added).astype(BF)
        copy = pltpu.make_async_copy(out_buf.at[now], out_ref.at[now], sems.at[part])
        copy.start()
        copies.append(copy)
    for copy in copies:
        copy.wait()


def params(mebibytes):
    return pltpu.CompilerParams(vmem_limit_bytes=mebibytes * 1024 * 1024)


SMALL = pl.CostEstimate(flops=1_000_000, bytes_accessed=10_000, transcendentals=1_000)


def sorted_kernel(queries_ref, pairs_ref, out_ref, q_buf, kv_buf, out_buf, in_sems, out_sems):
    width, quarter = HEADS * HD, KVH // 2
    arrive = [pltpu.make_async_copy(pairs_ref.at[0], kv_buf, in_sems.at[4])]
    for part in range(4):
        now = pl.ds(part * quarter * width, quarter * width)
        arrive.append(pltpu.make_async_copy(queries_ref.at[0, :, now], q_buf.at[:, now], in_sems.at[part]))
    for copy in arrive:
        copy.start()
    arrive[0].wait()
    leave = []
    for part in range(4):
        arrive[part + 1].wait()
        for to in range(part * quarter, (part + 1) * quarter):
            group = to // 2
            out_buf[to, :, :width] = q_buf[:, to * width : (to + 1) * width]
            out_buf[to, :, width:] = kv_buf[:, group * 2 * HD : (group + 1) * 2 * HD]
        now = pl.ds(part * quarter, quarter)
        leave.append(pltpu.make_async_copy(out_buf.at[now], out_ref.at[now], out_sems.at[part]))
        leave[-1].start()
    for copy in leave:
        copy.wait()


def sorted_part(queries, pairs):
    shape = (2 * KVH, queries.shape[1], (HEADS + 2) * HD)
    return pl.pallas_call(
        sorted_kernel,
        out_shape=jax.ShapeDtypeStruct(shape, BF),
        in_specs=[ANY, ANY],
        out_specs=ANY,
        scratch_shapes=[
            pltpu.VMEM(queries.shape[1:], BF),
            pltpu.VMEM(pairs.shape[1:], BF),
            pltpu.VMEM(shape, BF),
            pltpu.SemaphoreType.DMA((5,)),
            pltpu.SemaphoreType.DMA((4,)),
        ],
        compiler_params=params(60),
    )(queries, pairs)


def own_part(table, query_rows, lower, upper):
    return pl.pallas_call(
        own_kernel,
        out_shape=STATE,
        in_specs=[SMEM] + [VMEM] * 3,
        out_specs=[VMEM] * 2,
        scratch_shapes=buffers(PIECES),
        compiler_params=params(16),
    )(table, query_rows, lower, upper)


def more_part(table, query_rows, fill, blocks, state):
    return pl.pallas_call(
        more_kernel,
        out_shape=STATE,
        in_specs=[SMEM] + [VMEM] * (4 + len(blocks)),
        out_specs=[VMEM] * 2,
        scratch_shapes=buffers(2 * PIECES),
        cost_estimate=SMALL,
        compiler_params=params(16),
    )(table, query_rows, fill, *blocks, *state)


def last_part(table, query_rows, fill, blocks, state, kept_local, router, residual):
    return pl.pallas_call(
        last_kernel,
        out_shape=jax.ShapeDtypeStruct((TOK_DEV, HEADS * HD), BF),
        in_specs=[SMEM] + [VMEM] * 9 + [ANY],
        out_specs=ANY,
        scratch_shapes=buffers(PIECES)
        + [pltpu.VMEM(s.shape, s.dtype) for s in STATE]
        + [pltpu.VMEM((TOK_DEV, HEADS * HD), BF)] * 2
        + [pltpu.SemaphoreType.DMA((5,))],
        compiler_params=params(16),
    )(table, query_rows, fill, *blocks, *state, kept_local, router, residual)


def tables(kept_local, y, xl, co):
    own = (y * 2 + xl) * 2 + co
    counts = jnp.sum((kept_local < TOK_DEV).astype(jnp.int32), axis=1)
    at = jnp.arange(4 * PIECES, dtype=jnp.int32)
    group, piece = at // PIECES, at % PIECES
    straight = (piece // 2) ^ (piece // 4)
    split = jnp.where(piece < 4, piece // 2, jnp.where((piece == 4) | (piece == 7), 2, 3))
    behind = jnp.where(group < 2, straight, split)
    half = jnp.where((group < 2) | (piece < 4), piece % 2, jnp.where(piece == 5, 0, piece // 6))
    block = (((y - behind + 4) % 4) * 2 + (xl ^ (group // 2))) * 2 + (co ^ (group % 2))
    block_count = jnp.sum(jnp.where(block[:, None] == jnp.arange(N_CTX), counts[None, :], 0), axis=1)
    live = jnp.where(block < own, jnp.clip(block_count - half * HALF, 0, HALF), 0)
    taken = (live + GRAN - 1) // GRAN * GRAN
    part = (group + 1) // 2
    to = jnp.arange(PIECES_ALL + 3, dtype=jnp.int32)[:, None]
    to_part = jnp.where(to < PIECES_ALL, (to // PIECES + 1) // 2, to - PIECES_ALL)
    counted = (to_part == part[None, :]) & (at[None, :] < to)
    offset = jnp.sum(jnp.where(counted, taken[None, :], 0), axis=1)
    return jnp.concatenate([live, offset, jnp.broadcast_to(own, (1,))]).astype(jnp.int32)


def shards(residual, queries, keys_values, kept_local, router_weight):
    y, xl, co = (lax.axis_index(a) for a in CTX)
    sent = sorted_part(queries, keys_values)
    sent = lax.all_to_all(sent, TP, split_axis=0, concat_axis=0, tiled=True)
    sent = sent.reshape(CAP, (HEADS + 2) * HD)
    query_rows, pairs = sent[:, : HEADS * HD], sent[:, HEADS * HD :]
    table = tables(kept_local, y, xl, co)
    router = jnp.broadcast_to(router_weight[0].astype(F32)[:, None], (CAP, HD))
    pairs, table, router = lax.optimization_barrier((pairs, table, router))

    behind_1, behind_3, behind_2 = (shift(pairs, "y", d) for d in (1, 3, 2))
    own_x = shift_x(pairs, 1)
    lower = jnp.concatenate([pairs, behind_1], axis=0)
    upper = jnp.concatenate([behind_3, behind_2], axis=0)
    lower_x = shift_x(jnp.concatenate([behind_1, behind_2[:HALF]], axis=0), 1)
    upper_x = shift_x(jnp.concatenate([behind_3, behind_2[HALF:]], axis=0), 3)
    state = own_part(table, query_rows, lower, upper)
    low, up, *state = lax.optimization_barrier((lower, upper, *state))
    others = [shift(low, "co", 1), shift(up, "co", 1)]
    own_x, lower_x, upper_x, *state = lax.optimization_barrier((own_x, lower_x, upper_x, *state))
    arrived = [own_x, lower_x, upper_x]
    swapped = [shift(x, "co", 1) for x in arrived]
    state = more_part(table, query_rows, pairs, [*others, *arrived], state)
    return last_part(table, query_rows, pairs, swapped, state, kept_local, router, residual)


def solution(mesh):
    grid = Mesh(mesh.devices.reshape(4, 2, 2, 8, 2), CTX + TP)
    placed = (P(CTX, TP), P(CTX, TP, None), P(CTX, TP, None), P(), P(CTX, None))
    return jax.shard_map(shards, mesh=grid, in_specs=placed, out_specs=P(CTX, TP), check_vma=False)
```

```python
import math

import jax
import jax.numpy as jnp
from jax import lax
from jax.experimental import pallas as pl
from jax.experimental.pallas import tpu as pltpu
from jax.sharding import Mesh, PartitionSpec as P

H = 64
KVH = 8
HD = 128
TOK_DEV = 1024
CAP = 256
N_CTX = 16
HEADS = 4
ROWS = HEADS * CAP
HALF = 128
GRAN = 16
TILE = 256
PIECES = 8
PIECES_ALL = 4 * PIECES
FIRST = (0, PIECES, 3 * PIECES, 4 * PIECES)
CTX = ("y", "xl", "co")
TP = ("z", "xh")
BF = jnp.bfloat16
F32 = jnp.float32
HIDDEN = -1e30
EXP2_SCALE = math.log2(math.e) / math.sqrt(HD)
CONTRACT_LAST = (((1,), (1,)), ((), ()))
VMEM = pl.BlockSpec(memory_space=pltpu.VMEM)
SMEM = pl.BlockSpec(memory_space=pltpu.SMEM)
ANY = pl.BlockSpec(memory_space=pltpu.HBM)
STATE = [jax.ShapeDtypeStruct((ROWS, HD), F32), jax.ShapeDtypeStruct((ROWS, 2 * HD), F32)]


def buffers(pieces):
    rows = pieces * HALF + TILE
    return [pltpu.VMEM((rows, HD), BF), pltpu.VMEM((rows, 2 * HD), BF)]


def shift(block, axis, distance):
    size = lax.axis_size(axis)
    return lax.ppermute(block, axis, [(i, (i + distance) % size) for i in range(size)])


def shift_x(block, distance):
    def at(x):
        return (x % 2) * 2 + x // 2

    return lax.ppermute(block, ("xl", "xh"), [(at(x), at((x + distance) % 4)) for x in range(4)])


def compact(pieces, group, table_ref, fill_ref, k_buf, v_buf):
    row_in = lax.broadcasted_iota(jnp.int32, (HALF, HD), 0)
    fill = jnp.broadcast_to(fill_ref[:GRAN, :HD][0:1], (HALF, HD))
    for at, (piece, first) in enumerate(pieces):
        start = pl.multiple_of(table_ref[PIECES_ALL + FIRST[group] + at], GRAN)
        live = table_ref[FIRST[group] + at]
        rows, now = pl.ds(start, HALF), slice(first, first + HALF)

        @pl.when(live > 0)
        def _():
            inside = row_in < live
            k_buf[rows, :] = jnp.where(inside, piece[now, :HD], fill)
            v_buf[rows, :HD] = jnp.where(inside, piece[now, HD:], jnp.zeros((HALF, HD), BF))
            v_buf[rows, HD:] = jnp.where(inside, 1.0, 0.0).astype(BF)

    end = pl.multiple_of(table_ref[2 * PIECES_ALL + group], GRAN)
    k_buf[pl.ds(end, TILE), :] = jnp.concatenate([fill] * (TILE // HALF), axis=0)
    v_buf[pl.ds(end, TILE), :] = jnp.zeros((TILE, 2 * HD), BF)
    return (end + TILE - 1) // TILE


def twice(column):
    return jnp.concatenate([column, column], axis=1)


def soften(scores, before):
    top = before
    for lane in range(0, scores.shape[1], HD):
        now = scores[:, lane : lane + HD]
        top = now if top is None else jnp.maximum(top, now)
    top = jnp.broadcast_to(jnp.max(top, axis=1, keepdims=True), (CAP, HD))
    shifted = top * EXP2_SCALE
    shifted = jnp.concatenate([shifted] * (scores.shape[1] // HD), axis=1)
    return top, jnp.exp2(scores * EXP2_SCALE - shifted).astype(BF)


def absorb(tiles, q_ref, k_buf, v_buf, old, new):
    (top_old, sum_old), (top_new, sum_new) = old, new
    for count in range((k_buf.shape[0] - TILE) // TILE + 1):

        @pl.when(tiles == count)
        def _():
            if count == 0:
                top_new[...] = top_old[...]
                sum_new[...] = sum_old[...]
                return
            keys = count * TILE
            for head in range(HEADS):
                now = slice(head * CAP, (head + 1) * CAP)
                query = q_ref[:, head * HD : (head + 1) * HD]
                scores = lax.dot_general(
                    query, k_buf[:keys, :], CONTRACT_LAST, preferred_element_type=F32
                )
                before = top_old[now, :]
                top, weights = soften(scores, before)
                factor = jnp.exp2((before - top) * EXP2_SCALE)
                added = jnp.dot(weights, v_buf[:keys, :], preferred_element_type=F32)
                sum_new[now, :] = sum_old[now, :] * twice(factor) + added
                top_new[now, :] = top


def pieces_of(*refs):
    return [(ref, row) for ref in refs for row in range(0, ref.shape[0], HALF)]


def own_kernel(table_ref, q_ref, lower_ref, upper_ref, top_ref, sum_ref, k_buf, v_buf):
    rows = lax.broadcasted_iota(jnp.int32, (CAP, CAP), 0)
    cols = lax.broadcasted_iota(jnp.int32, (CAP, CAP), 1)
    tiles = compact(pieces_of(lower_ref, upper_ref), 0, table_ref, lower_ref, k_buf, v_buf)
    keys = lower_ref[:CAP, :HD]
    values = jnp.concatenate([lower_ref[:CAP, HD:], jnp.ones((CAP, HD), BF)], axis=1)
    for head in range(HEADS):
        now = slice(head * CAP, (head + 1) * CAP)
        query = q_ref[:, head * HD : (head + 1) * HD]
        scores = lax.dot_general(query, keys, CONTRACT_LAST, preferred_element_type=F32)
        top, weights = soften(jnp.where(cols <= rows, scores, HIDDEN), None)
        top_ref[now, :] = top
        sum_ref[now, :] = jnp.dot(weights, values, preferred_element_type=F32)
    state = (top_ref, sum_ref)
    absorb(tiles, q_ref, k_buf, v_buf, state, state)


def more_kernel(table_ref, q_ref, fill_ref, *rest):
    blocks, state, (top_ref, sum_ref, k_buf, v_buf) = rest[:-6], rest[-6:-4], rest[-4:]
    tiles = compact(pieces_of(*blocks), 1, table_ref, fill_ref, k_buf, v_buf)
    absorb(tiles, q_ref, k_buf, v_buf, state, (top_ref, sum_ref))


def last_kernel(table_ref, q_ref, fill_ref, own_ref, lower_ref, upper_ref, top0, sum0, kept_ref, router_ref, residual_ref, out_ref, k_buf, v_buf, top_ref, sum_ref, residual_buf, out_buf, sems):
    fetch = pltpu.make_async_copy(residual_ref, residual_buf, sems.at[4])
    fetch.start()
    pieces = pieces_of(own_ref, lower_ref, upper_ref)
    tiles = compact(pieces, 2, table_ref, fill_ref, k_buf, v_buf)
    absorb(tiles, q_ref, k_buf, v_buf, (top0, sum0), (top_ref, sum_ref))
    updates = []
    for head in range(HEADS):
        now = slice(head * CAP, (head + 1) * CAP)
        attention = sum_ref[now, :HD] / sum_ref[now, HD:]
        updates.append((router_ref[...] * attention).astype(BF))
    update = jnp.concatenate(updates, axis=1)
    kept = kept_ref[pl.ds(table_ref[2 * PIECES_ALL + 3], 1), :]
    fetch.wait()
    copies = []
    for part, row in enumerate(range(0, TOK_DEV, CAP)):
        now = slice(row, row + CAP)
        place = lax.broadcasted_iota(jnp.int32, (CAP, CAP), 0) + row
        chosen = jnp.where(place == kept, 1.0, 0.0).astype(BF)
        added = jnp.dot(chosen, update, preferred_element_type=F32)
        out_buf[now, :] = (residual_buf[now, :].astype(F32) + added).astype(BF)
        copy = pltpu.make_async_copy(out_buf.at[now], out_ref.at[now], sems.at[part])
        copy.start()
        copies.append(copy)
    for copy in copies:
        copy.wait()


def params(mebibytes):
    return pltpu.CompilerParams(vmem_limit_bytes=mebibytes * 1024 * 1024)


SMALL = pl.CostEstimate(flops=1_000_000, bytes_accessed=10_000, transcendentals=1_000)


def sorted_kernel(queries_ref, pairs_ref, out_ref, q_buf, kv_buf, out_buf, in_sems, out_sems):
    width, quarter = HEADS * HD, KVH // 2
    arrive = [pltpu.make_async_copy(pairs_ref.at[0], kv_buf, in_sems.at[4])]
    for part in range(4):
        now = pl.ds(part * quarter * width, quarter * width)
        arrive.append(pltpu.make_async_copy(queries_ref.at[0, :, now], q_buf.at[:, now], in_sems.at[part]))
    for copy in arrive:
        copy.start()
    arrive[0].wait()
    leave = []
    for part in range(4):
        arrive[part + 1].wait()
        for to in range(part * quarter, (part + 1) * quarter):
            group = to // 2
            out_buf[to, :, :width] = q_buf[:, to * width : (to + 1) * width]
            out_buf[to, :, width:] = kv_buf[:, group * 2 * HD : (group + 1) * 2 * HD]
        now = pl.ds(part * quarter, quarter)
        leave.append(pltpu.make_async_copy(out_buf.at[now], out_ref.at[now], out_sems.at[part]))
        leave[-1].start()
    for copy in leave:
        copy.wait()


def sorted_part(queries, pairs):
    shape = (2 * KVH, queries.shape[1], (HEADS + 2) * HD)
    return pl.pallas_call(
        sorted_kernel,
        out_shape=jax.ShapeDtypeStruct(shape, BF),
        in_specs=[ANY, ANY],
        out_specs=ANY,
        scratch_shapes=[
            pltpu.VMEM(queries.shape[1:], BF),
            pltpu.VMEM(pairs.shape[1:], BF),
            pltpu.VMEM(shape, BF),
            pltpu.SemaphoreType.DMA((5,)),
            pltpu.SemaphoreType.DMA((4,)),
        ],
        compiler_params=params(60),
    )(queries, pairs)


def own_part(table, query_rows, lower, upper):
    return pl.pallas_call(
        own_kernel,
        out_shape=STATE,
        in_specs=[SMEM] + [VMEM] * 3,
        out_specs=[VMEM] * 2,
        scratch_shapes=buffers(PIECES),
        compiler_params=params(16),
    )(table, query_rows, lower, upper)


def more_part(table, query_rows, fill, blocks, state):
    return pl.pallas_call(
        more_kernel,
        out_shape=STATE,
        in_specs=[SMEM] + [VMEM] * (4 + len(blocks)),
        out_specs=[VMEM] * 2,
        scratch_shapes=buffers(2 * PIECES),
        cost_estimate=SMALL,
        compiler_params=params(16),
    )(table, query_rows, fill, *blocks, *state)


def last_part(table, query_rows, fill, blocks, state, kept_local, router, residual):
    return pl.pallas_call(
        last_kernel,
        out_shape=jax.ShapeDtypeStruct((TOK_DEV, HEADS * HD), BF),
        in_specs=[SMEM] + [VMEM] * 9 + [ANY],
        out_specs=ANY,
        scratch_shapes=buffers(PIECES)
        + [pltpu.VMEM(s.shape, s.dtype) for s in STATE]
        + [pltpu.VMEM((TOK_DEV, HEADS * HD), BF)] * 2
        + [pltpu.SemaphoreType.DMA((5,))],
        compiler_params=params(16),
    )(table, query_rows, fill, *blocks, *state, kept_local, router, residual)


def tables(kept_local, y, xl, co):
    own = (y * 2 + xl) * 2 + co
    counts = jnp.sum((kept_local < TOK_DEV).astype(jnp.int32), axis=1)
    at = jnp.arange(4 * PIECES, dtype=jnp.int32)
    group, piece = at // PIECES, at % PIECES
    straight = (piece // 2) ^ (piece // 4)
    split = jnp.where(piece < 4, piece // 2, jnp.where((piece == 4) | (piece == 7), 2, 3))
    behind = jnp.where(group < 2, straight, split)
    half = jnp.where((group < 2) | (piece < 4), piece % 2, jnp.where(piece == 5, 0, piece // 6))
    block = (((y - behind + 4) % 4) * 2 + (xl ^ (group // 2))) * 2 + (co ^ (group % 2))
    block_count = jnp.sum(jnp.where(block[:, None] == jnp.arange(N_CTX), counts[None, :], 0), axis=1)
    live = jnp.where(block < own, jnp.clip(block_count - half * HALF, 0, HALF), 0)
    taken = (live + GRAN - 1) // GRAN * GRAN
    part = (group + 1) // 2
    to = jnp.arange(PIECES_ALL + 3, dtype=jnp.int32)[:, None]
    to_part = jnp.where(to < PIECES_ALL, (to // PIECES + 1) // 2, to - PIECES_ALL)
    counted = (to_part == part[None, :]) & (at[None, :] < to)
    offset = jnp.sum(jnp.where(counted, taken[None, :], 0), axis=1)
    return jnp.concatenate([live, offset, jnp.broadcast_to(own, (1,))]).astype(jnp.int32)


def shards(residual, queries, keys_values, kept_local, router_weight):
    y, xl, co = (lax.axis_index(a) for a in CTX)
    sent = sorted_part(queries, keys_values)
    sent = lax.all_to_all(sent, TP, split_axis=0, concat_axis=0, tiled=True)
    sent = sent.reshape(CAP, (HEADS + 2) * HD)
    query_rows, pairs = sent[:, : HEADS * HD], sent[:, HEADS * HD :]
    table = tables(kept_local, y, xl, co)
    router = jnp.broadcast_to(router_weight[0].astype(F32)[:, None], (CAP, HD))
    pairs, table, router = lax.optimization_barrier((pairs, table, router))

    behind_1, behind_3, behind_2 = (shift(pairs, "y", d) for d in (1, 3, 2))
    own_x = shift_x(pairs, 1)
    lower = jnp.concatenate([pairs, behind_1], axis=0)
    upper = jnp.concatenate([behind_3, behind_2], axis=0)
    lower_x = shift_x(jnp.concatenate([behind_1, behind_2[:HALF]], axis=0), 1)
    upper_x = shift_x(jnp.concatenate([behind_3, behind_2[HALF:]], axis=0), 3)
    state = own_part(table, query_rows, lower, upper)
    low, up, *state = lax.optimization_barrier((lower, upper, *state))
    others = [shift(low, "co", 1), shift(up, "co", 1)]
    own_x, lower_x, upper_x, *state = lax.optimization_barrier((own_x, lower_x, upper_x, *state))
    arrived = [own_x, lower_x, upper_x]
    swapped = [shift(x, "co", 1) for x in arrived]
    state = more_part(table, query_rows, pairs, [*others, *arrived], state)
    return last_part(table, query_rows, pairs, swapped, state, kept_local, router, residual)


def solution(mesh):
    grid = Mesh(mesh.devices.reshape(4, 2, 2, 8, 2), CTX + TP)
    placed = (P(CTX, TP), P(CTX, TP, None), P(CTX, TP, None), P(), P(CTX, None))
    return jax.shard_map(shards, mesh=grid, in_specs=placed, out_specs=P(CTX, TP), check_vma=False)
```

```python
import math

import jax
import jax.numpy as jnp
from jax import lax
from jax.experimental import pallas as pl
from jax.experimental.pallas import tpu as pltpu
from jax.sharding import Mesh, PartitionSpec as P

H = 64
KVH = 8
HD = 128
TOK_DEV = 1024
CAP = 256
N_CTX = 16
HEADS = 4
ROWS = HEADS * CAP
HALF = 128
GRAN = 16
TILE = 256
PIECES = 8
PIECES_ALL = 4 * PIECES
FIRST = (0, PIECES, 3 * PIECES, 4 * PIECES)
CTX = ("y", "xl", "co")
TP = ("z", "xh")
BF = jnp.bfloat16
F32 = jnp.float32
HIDDEN = -1e30
EXP2_SCALE = math.log2(math.e) / math.sqrt(HD)
CONTRACT_LAST = (((1,), (1,)), ((), ()))
VMEM = pl.BlockSpec(memory_space=pltpu.VMEM)
SMEM = pl.BlockSpec(memory_space=pltpu.SMEM)
ANY = pl.BlockSpec(memory_space=pltpu.HBM)
STATE = [jax.ShapeDtypeStruct((ROWS, HD), F32), jax.ShapeDtypeStruct((ROWS, 2 * HD), F32)]


def buffers(pieces):
    rows = pieces * HALF + TILE
    return [pltpu.VMEM((rows, HD), BF), pltpu.VMEM((rows, 2 * HD), BF)]


def shift(block, axis, distance):
    size = lax.axis_size(axis)
    return lax.ppermute(block, axis, [(i, (i + distance) % size) for i in range(size)])


def shift_x(block, distance):
    def at(x):
        return (x % 2) * 2 + x // 2

    return lax.ppermute(block, ("xl", "xh"), [(at(x), at((x + distance) % 4)) for x in range(4)])


def compact(pieces, group, table_ref, fill_ref, k_buf, v_buf):
    row_in = lax.broadcasted_iota(jnp.int32, (HALF, HD), 0)
    fill = jnp.broadcast_to(fill_ref[:GRAN, :HD][0:1], (HALF, HD))
    for at, (piece, first) in enumerate(pieces):
        start = pl.multiple_of(table_ref[PIECES_ALL + FIRST[group] + at], GRAN)
        live = table_ref[FIRST[group] + at]
        rows, now = pl.ds(start, HALF), slice(first, first + HALF)

        @pl.when(live > 0)
        def _():
            inside = row_in < live
            k_buf[rows, :] = jnp.where(inside, piece[now, :HD], fill)
            v_buf[rows, :HD] = jnp.where(inside, piece[now, HD:], jnp.zeros((HALF, HD), BF))
            v_buf[rows, HD:] = jnp.where(inside, 1.0, 0.0).astype(BF)

    end = pl.multiple_of(table_ref[2 * PIECES_ALL + group], GRAN)
    k_buf[pl.ds(end, TILE), :] = jnp.concatenate([fill] * (TILE // HALF), axis=0)
    v_buf[pl.ds(end, TILE), :] = jnp.zeros((TILE, 2 * HD), BF)
    return (end + TILE - 1) // TILE


def twice(column):
    return jnp.concatenate([column, column], axis=1)


def soften(scores, before):
    top = before
    for lane in range(0, scores.shape[1], HD):
        now = scores[:, lane : lane + HD]
        top = now if top is None else jnp.maximum(top, now)
    top = jnp.broadcast_to(jnp.max(top, axis=1, keepdims=True), (CAP, HD))
    shifted = top * EXP2_SCALE
    shifted = jnp.concatenate([shifted] * (scores.shape[1] // HD), axis=1)
    return top, jnp.exp2(scores * EXP2_SCALE - shifted).astype(BF)


def absorb(tiles, q_ref, k_buf, v_buf, old, new):
    (top_old, sum_old), (top_new, sum_new) = old, new
    for count in range((k_buf.shape[0] - TILE) // TILE + 1):

        @pl.when(tiles == count)
        def _():
            if count == 0:
                if old is new:
                    return
                top_new[...] = top_old[...]
                sum_new[...] = sum_old[...]
                return
            keys = count * TILE
            for head in range(HEADS):
                now = slice(head * CAP, (head + 1) * CAP)
                query = q_ref[:, head * HD : (head + 1) * HD]
                scores = lax.dot_general(
                    query, k_buf[:keys, :], CONTRACT_LAST, preferred_element_type=F32
                )
                before = top_old[now, :]
                top, weights = soften(scores, before)
                factor = jnp.exp2((before - top) * EXP2_SCALE)
                added = jnp.dot(weights, v_buf[:keys, :], preferred_element_type=F32)
                sum_new[now, :] = sum_old[now, :] * twice(factor) + added
                top_new[now, :] = top


def pieces_of(*refs):
    return [(ref, row) for ref in refs for row in range(0, ref.shape[0], HALF)]


def own_kernel(table_ref, q_ref, lower_ref, upper_ref, top_ref, sum_ref, k_buf, v_buf):
    rows = lax.broadcasted_iota(jnp.int32, (CAP, CAP), 0)
    cols = lax.broadcasted_iota(jnp.int32, (CAP, CAP), 1)
    tiles = compact(pieces_of(lower_ref, upper_ref), 0, table_ref, lower_ref, k_buf, v_buf)
    keys = lower_ref[:CAP, :HD]
    values = jnp.concatenate([lower_ref[:CAP, HD:], jnp.ones((CAP, HD), BF)], axis=1)
    for head in range(HEADS):
        now = slice(head * CAP, (head + 1) * CAP)
        query = q_ref[:, head * HD : (head + 1) * HD]
        scores = lax.dot_general(query, keys, CONTRACT_LAST, preferred_element_type=F32)
        top, weights = soften(jnp.where(cols <= rows, scores, HIDDEN), None)
        top_ref[now, :] = top
        sum_ref[now, :] = jnp.dot(weights, values, preferred_element_type=F32)
    state = (top_ref, sum_ref)
    absorb(tiles, q_ref, k_buf, v_buf, state, state)


def more_kernel(table_ref, q_ref, fill_ref, *rest):
    blocks, state, (top_ref, sum_ref, k_buf, v_buf) = rest[:-6], rest[-6:-4], rest[-4:]
    tiles = compact(pieces_of(*blocks), 1, table_ref, fill_ref, k_buf, v_buf)
    absorb(tiles, q_ref, k_buf, v_buf, state, (top_ref, sum_ref))


def last_kernel(table_ref, q_ref, fill_ref, own_ref, lower_ref, upper_ref, top0, sum0, kept_ref, router_ref, residual_ref, out_ref, top_ref, sum_ref, k_buf, v_buf, residual_buf, out_buf, sems):
    fetch = pltpu.make_async_copy(residual_ref, residual_buf, sems.at[4])
    fetch.start()
    pieces = pieces_of(own_ref, lower_ref, upper_ref)
    tiles = compact(pieces, 2, table_ref, fill_ref, k_buf, v_buf)
    state = (top_ref, sum_ref)
    absorb(tiles, q_ref, k_buf, v_buf, state, state)
    updates = []
    for head in range(HEADS):
        now = slice(head * CAP, (head + 1) * CAP)
        attention = sum_ref[now, :HD] / sum_ref[now, HD:]
        updates.append((router_ref[...] * attention).astype(BF))
    update = jnp.concatenate(updates, axis=1)
    kept = kept_ref[pl.ds(table_ref[2 * PIECES_ALL + 3], 1), :]
    fetch.wait()
    copies = []
    for part, row in enumerate(range(0, TOK_DEV, CAP)):
        now = slice(row, row + CAP)
        place = lax.broadcasted_iota(jnp.int32, (CAP, CAP), 0) + row
        chosen = jnp.where(place == kept, 1.0, 0.0).astype(BF)
        added = jnp.dot(chosen, update, preferred_element_type=F32)
        out_buf[now, :] = (residual_buf[now, :].astype(F32) + added).astype(BF)
        copy = pltpu.make_async_copy(out_buf.at[now], out_ref.at[now], sems.at[part])
        copy.start()
        copies.append(copy)
    for copy in copies:
        copy.wait()


def params(mebibytes):
    return pltpu.CompilerParams(vmem_limit_bytes=mebibytes * 1024 * 1024)


SMALL = pl.CostEstimate(flops=1_000_000, bytes_accessed=10_000, transcendentals=1_000)


def sorted_kernel(queries_ref, pairs_ref, out_ref, q_buf, kv_buf, out_buf, in_sems, out_sems):
    width, quarter = HEADS * HD, KVH // 2
    arrive = [pltpu.make_async_copy(pairs_ref.at[0], kv_buf, in_sems.at[4])]
    for part in range(4):
        now = pl.ds(part * quarter * width, quarter * width)
        arrive.append(pltpu.make_async_copy(queries_ref.at[0, :, now], q_buf.at[:, now], in_sems.at[part]))
    for copy in arrive:
        copy.start()
    arrive[0].wait()
    leave = []
    for part in range(4):
        arrive[part + 1].wait()
        for to in range(part * quarter, (part + 1) * quarter):
            group = to // 2
            out_buf[to, :, :width] = q_buf[:, to * width : (to + 1) * width]
            out_buf[to, :, width:] = kv_buf[:, group * 2 * HD : (group + 1) * 2 * HD]
        now = pl.ds(part * quarter, quarter)
        leave.append(pltpu.make_async_copy(out_buf.at[now], out_ref.at[now], out_sems.at[part]))
        leave[-1].start()
    for copy in leave:
        copy.wait()


def sorted_part(queries, pairs):
    shape = (2 * KVH, queries.shape[1], (HEADS + 2) * HD)
    return pl.pallas_call(
        sorted_kernel,
        out_shape=jax.ShapeDtypeStruct(shape, BF),
        in_specs=[ANY, ANY],
        out_specs=ANY,
        scratch_shapes=[
            pltpu.VMEM(queries.shape[1:], BF),
            pltpu.VMEM(pairs.shape[1:], BF),
            pltpu.VMEM(shape, BF),
            pltpu.SemaphoreType.DMA((5,)),
            pltpu.SemaphoreType.DMA((4,)),
        ],
        compiler_params=params(60),
    )(queries, pairs)


def own_part(table, query_rows, lower, upper):
    return pl.pallas_call(
        own_kernel,
        out_shape=STATE,
        in_specs=[SMEM] + [VMEM] * 3,
        out_specs=[VMEM] * 2,
        scratch_shapes=buffers(PIECES),
        compiler_params=params(16),
    )(table, query_rows, lower, upper)


def more_part(table, query_rows, fill, blocks, state):
    return pl.pallas_call(
        more_kernel,
        out_shape=STATE,
        in_specs=[SMEM] + [VMEM] * (4 + len(blocks)),
        out_specs=[VMEM] * 2,
        scratch_shapes=buffers(2 * PIECES),
        cost_estimate=SMALL,
        compiler_params=params(16),
    )(table, query_rows, fill, *blocks, *state)


def last_part(table, query_rows, fill, blocks, state, kept_local, router, residual):
    return pl.pallas_call(
        last_kernel,
        out_shape=[jax.ShapeDtypeStruct((TOK_DEV, HEADS * HD), BF), *STATE],
        in_specs=[SMEM] + [VMEM] * 9 + [ANY],
        out_specs=[ANY, VMEM, VMEM],
        input_output_aliases={3 + len(blocks): 1, 4 + len(blocks): 2},
        scratch_shapes=buffers(PIECES)
        + [pltpu.VMEM((TOK_DEV, HEADS * HD), BF)] * 2
        + [pltpu.SemaphoreType.DMA((5,))],
        compiler_params=params(16),
    )(table, query_rows, fill, *blocks, *state, kept_local, router, residual)[0]


def tables(kept_local, y, xl, co):
    own = (y * 2 + xl) * 2 + co
    counts = jnp.sum((kept_local < TOK_DEV).astype(jnp.int32), axis=1)
    at = jnp.arange(4 * PIECES, dtype=jnp.int32)
    group, piece = at // PIECES, at % PIECES
    straight = (piece // 2) ^ (piece // 4)
    split = jnp.where(piece < 4, piece // 2, jnp.where((piece == 4) | (piece == 7), 2, 3))
    behind = jnp.where(group < 2, straight, split)
    half = jnp.where((group < 2) | (piece < 4), piece % 2, jnp.where(piece == 5, 0, piece // 6))
    block = (((y - behind + 4) % 4) * 2 + (xl ^ (group // 2))) * 2 + (co ^ (group % 2))
    block_count = jnp.sum(jnp.where(block[:, None] == jnp.arange(N_CTX), counts[None, :], 0), axis=1)
    live = jnp.where(block < own, jnp.clip(block_count - half * HALF, 0, HALF), 0)
    taken = (live + GRAN - 1) // GRAN * GRAN
    part = (group + 1) // 2
    to = jnp.arange(PIECES_ALL + 3, dtype=jnp.int32)[:, None]
    to_part = jnp.where(to < PIECES_ALL, (to // PIECES + 1) // 2, to - PIECES_ALL)
    counted = (to_part == part[None, :]) & (at[None, :] < to)
    offset = jnp.sum(jnp.where(counted, taken[None, :], 0), axis=1)
    return jnp.concatenate([live, offset, jnp.broadcast_to(own, (1,))]).astype(jnp.int32)


def shards(residual, queries, keys_values, kept_local, router_weight):
    y, xl, co = (lax.axis_index(a) for a in CTX)
    sent = sorted_part(queries, keys_values)
    sent = lax.all_to_all(sent, TP, split_axis=0, concat_axis=0, tiled=True)
    sent = sent.reshape(CAP, (HEADS + 2) * HD)
    query_rows, pairs = sent[:, : HEADS * HD], sent[:, HEADS * HD :]
    table = tables(kept_local, y, xl, co)
    router = jnp.broadcast_to(router_weight[0].astype(F32)[:, None], (CAP, HD))
    pairs, table, router = lax.optimization_barrier((pairs, table, router))

    behind_1, behind_3, behind_2 = (shift(pairs, "y", d) for d in (1, 3, 2))
    own_x = shift_x(pairs, 1)
    lower = jnp.concatenate([pairs, behind_1], axis=0)
    upper = jnp.concatenate([behind_3, behind_2], axis=0)
    lower_x = shift_x(jnp.concatenate([behind_1, behind_2[:HALF]], axis=0), 1)
    upper_x = shift_x(jnp.concatenate([behind_3, behind_2[HALF:]], axis=0), 3)
    state = own_part(table, query_rows, lower, upper)
    low, up, *state = lax.optimization_barrier((lower, upper, *state))
    others = [shift(low, "co", 1), shift(up, "co", 1)]
    own_x, lower_x, upper_x, *state = lax.optimization_barrier((own_x, lower_x, upper_x, *state))
    arrived = [own_x, lower_x, upper_x]
    swapped = [shift(x, "co", 1) for x in arrived]
    state = more_part(table, query_rows, pairs, [*others, *arrived], state)
    return last_part(table, query_rows, pairs, swapped, state, kept_local, router, residual)


def solution(mesh):
    grid = Mesh(mesh.devices.reshape(4, 2, 2, 8, 2), CTX + TP)
    placed = (P(CTX, TP), P(CTX, TP, None), P(CTX, TP, None), P(), P(CTX, None))
    return jax.shard_map(shards, mesh=grid, in_specs=placed, out_specs=P(CTX, TP), check_vma=False)
```

```python
import math

import jax
import jax.numpy as jnp
from jax import lax
from jax.experimental import pallas as pl
from jax.experimental.pallas import tpu as pltpu
from jax.sharding import Mesh, PartitionSpec as P

H = 64
KVH = 8
HD = 128
TOK_DEV = 1024
CAP = 256
N_CTX = 16
HEADS = 4
ROWS = HEADS * CAP
HALF = 128
GRAN = 16
TILE = 256
PIECES = 8
PIECES_ALL = 4 * PIECES
FIRST = (0, PIECES, 3 * PIECES, 4 * PIECES)
CTX = ("y", "xl", "co")
TP = ("z", "xh")
BF = jnp.bfloat16
F32 = jnp.float32
HIDDEN = -1e30
EXP2_SCALE = math.log2(math.e) / math.sqrt(HD)
CONTRACT_LAST = (((1,), (1,)), ((), ()))
VMEM = pl.BlockSpec(memory_space=pltpu.VMEM)
SMEM = pl.BlockSpec(memory_space=pltpu.SMEM)
ANY = pl.BlockSpec(memory_space=pltpu.HBM)
STATE = [jax.ShapeDtypeStruct((ROWS, HD), F32), jax.ShapeDtypeStruct((ROWS, 2 * HD), F32)]


def buffers(pieces):
    rows = pieces * HALF + TILE
    return [pltpu.VMEM((rows, HD), BF), pltpu.VMEM((rows, 2 * HD), BF)]


def shift(block, axis, distance):
    size = lax.axis_size(axis)
    return lax.ppermute(block, axis, [(i, (i + distance) % size) for i in range(size)])


def shift_x(block, distance):
    def at(x):
        return (x % 2) * 2 + x // 2

    return lax.ppermute(block, ("xl", "xh"), [(at(x), at((x + distance) % 4)) for x in range(4)])


def compact(pieces, group, table_ref, fill_ref, k_buf, v_buf):
    row_in = lax.broadcasted_iota(jnp.int32, (HALF, HD), 0)
    fill = jnp.broadcast_to(fill_ref[:GRAN, :HD][0:1], (HALF, HD))
    for at, (piece, first) in enumerate(pieces):
        start = pl.multiple_of(table_ref[PIECES_ALL + FIRST[group] + at], GRAN)
        live = table_ref[FIRST[group] + at]
        rows, now = pl.ds(start, HALF), slice(first, first + HALF)

        @pl.when(live > 0)
        def _():
            inside = row_in < live
            k_buf[rows, :] = jnp.where(inside, piece[now, :HD], fill)
            v_buf[rows, :HD] = jnp.where(inside, piece[now, HD:], jnp.zeros((HALF, HD), BF))
            v_buf[rows, HD:] = jnp.where(inside, 1.0, 0.0).astype(BF)

    end = pl.multiple_of(table_ref[2 * PIECES_ALL + group], GRAN)
    k_buf[pl.ds(end, TILE), :] = jnp.concatenate([fill] * (TILE // HALF), axis=0)
    v_buf[pl.ds(end, TILE), :] = jnp.zeros((TILE, 2 * HD), BF)
    return (end + TILE - 1) // TILE


def twice(column):
    return jnp.concatenate([column, column], axis=1)


def soften(scores, before):
    top = before
    for lane in range(0, scores.shape[1], HD):
        now = scores[:, lane : lane + HD]
        top = now if top is None else jnp.maximum(top, now)
    top = jnp.broadcast_to(jnp.max(top, axis=1, keepdims=True), (CAP, HD))
    shifted = top * EXP2_SCALE
    shifted = jnp.concatenate([shifted] * (scores.shape[1] // HD), axis=1)
    return top, jnp.exp2(scores * EXP2_SCALE - shifted).astype(BF)


def absorb(tiles, q_ref, k_buf, v_buf, old, new):
    (top_old, sum_old), (top_new, sum_new) = old, new
    for count in range((k_buf.shape[0] - TILE) // TILE + 1):

        @pl.when(tiles == count)
        def _():
            if count == 0:
                top_new[...] = top_old[...]
                sum_new[...] = sum_old[...]
                return
            keys = count * TILE
            for head in range(HEADS):
                now = slice(head * CAP, (head + 1) * CAP)
                query = q_ref[:, head * HD : (head + 1) * HD]
                scores = lax.dot_general(
                    query, k_buf[:keys, :], CONTRACT_LAST, preferred_element_type=F32
                )
                before = top_old[now, :]
                top, weights = soften(scores, before)
                factor = jnp.exp2((before - top) * EXP2_SCALE)
                added = jnp.dot(weights, v_buf[:keys, :], preferred_element_type=F32)
                sum_new[now, :] = sum_old[now, :] * twice(factor) + added
                top_new[now, :] = top


def pieces_of(*refs):
    return [(ref, row) for ref in refs for row in range(0, ref.shape[0], HALF)]


def own_kernel(table_ref, q_ref, lower_ref, upper_ref, top_ref, sum_ref, k_buf, v_buf):
    rows = lax.broadcasted_iota(jnp.int32, (CAP, CAP), 0)
    cols = lax.broadcasted_iota(jnp.int32, (CAP, CAP), 1)
    tiles = compact(pieces_of(lower_ref, upper_ref), 0, table_ref, lower_ref, k_buf, v_buf)
    keys = lower_ref[:CAP, :HD]
    values = jnp.concatenate([lower_ref[:CAP, HD:], jnp.ones((CAP, HD), BF)], axis=1)
    for head in range(HEADS):
        now = slice(head * CAP, (head + 1) * CAP)
        query = q_ref[:, head * HD : (head + 1) * HD]
        scores = lax.dot_general(query, keys, CONTRACT_LAST, preferred_element_type=F32)
        top, weights = soften(jnp.where(cols <= rows, scores, HIDDEN), None)
        top_ref[now, :] = top
        sum_ref[now, :] = jnp.dot(weights, values, preferred_element_type=F32)
    state = (top_ref, sum_ref)
    absorb(tiles, q_ref, k_buf, v_buf, state, state)


def more_kernel(table_ref, q_ref, fill_ref, *rest):
    blocks, state, (top_ref, sum_ref, k_buf, v_buf) = rest[:-6], rest[-6:-4], rest[-4:]
    tiles = compact(pieces_of(*blocks), 1, table_ref, fill_ref, k_buf, v_buf)
    absorb(tiles, q_ref, k_buf, v_buf, state, (top_ref, sum_ref))


def last_kernel(table_ref, q_ref, fill_ref, own_ref, lower_ref, upper_ref, top0, sum0, kept_ref, router_ref, residual_ref, out_ref, k_buf, v_buf, top_ref, sum_ref, residual_buf, out_buf, sems):
    fetch = pltpu.make_async_copy(residual_ref, residual_buf, sems.at[8])
    fetch.start()
    pieces = pieces_of(own_ref, lower_ref, upper_ref)
    tiles = compact(pieces, 2, table_ref, fill_ref, k_buf, v_buf)
    absorb(tiles, q_ref, k_buf, v_buf, (top0, sum0), (top_ref, sum_ref))
    updates = []
    for head in range(HEADS):
        now = slice(head * CAP, (head + 1) * CAP)
        attention = sum_ref[now, :HD] / sum_ref[now, HD:]
        updates.append((router_ref[...] * attention).astype(BF))
    update = jnp.concatenate(updates, axis=1)
    kept = kept_ref[pl.ds(table_ref[2 * PIECES_ALL + 3], 1), :]
    fetch.wait()
    copies = []
    for part, row in enumerate(range(0, TOK_DEV, HALF)):
        now = slice(row, row + HALF)
        place = lax.broadcasted_iota(jnp.int32, (HALF, CAP), 0) + row
        chosen = jnp.where(place == kept, 1.0, 0.0).astype(BF)
        added = jnp.dot(chosen, update, preferred_element_type=F32)
        out_buf[now, :] = (residual_buf[now, :].astype(F32) + added).astype(BF)
        copy = pltpu.make_async_copy(out_buf.at[now], out_ref.at[now], sems.at[part])
        copy.start()
        copies.append(copy)
    for copy in copies:
        copy.wait()


def params(mebibytes):
    return pltpu.CompilerParams(vmem_limit_bytes=mebibytes * 1024 * 1024)


SMALL = pl.CostEstimate(flops=1_000_000, bytes_accessed=10_000, transcendentals=1_000)


def sorted_kernel(queries_ref, pairs_ref, out_ref, q_buf, kv_buf, out_buf, in_sems, out_sems):
    width, quarter = HEADS * HD, KVH // 2
    arrive = [pltpu.make_async_copy(pairs_ref.at[0], kv_buf, in_sems.at[4])]
    for part in range(4):
        now = pl.ds(part * quarter * width, quarter * width)
        arrive.append(pltpu.make_async_copy(queries_ref.at[0, :, now], q_buf.at[:, now], in_sems.at[part]))
    for copy in arrive:
        copy.start()
    arrive[0].wait()
    leave = []
    for part in range(4):
        arrive[part + 1].wait()
        for to in range(part * quarter, (part + 1) * quarter):
            group = to // 2
            out_buf[to, :, :width] = q_buf[:, to * width : (to + 1) * width]
            out_buf[to, :, width:] = kv_buf[:, group * 2 * HD : (group + 1) * 2 * HD]
        now = pl.ds(part * quarter, quarter)
        leave.append(pltpu.make_async_copy(out_buf.at[now], out_ref.at[now], out_sems.at[part]))
        leave[-1].start()
    for copy in leave:
        copy.wait()


def sorted_part(queries, pairs):
    shape = (2 * KVH, queries.shape[1], (HEADS + 2) * HD)
    return pl.pallas_call(
        sorted_kernel,
        out_shape=jax.ShapeDtypeStruct(shape, BF),
        in_specs=[ANY, ANY],
        out_specs=ANY,
        scratch_shapes=[
            pltpu.VMEM(queries.shape[1:], BF),
            pltpu.VMEM(pairs.shape[1:], BF),
            pltpu.VMEM(shape, BF),
            pltpu.SemaphoreType.DMA((5,)),
            pltpu.SemaphoreType.DMA((4,)),
        ],
        compiler_params=params(60),
    )(queries, pairs)


def own_part(table, query_rows, lower, upper):
    return pl.pallas_call(
        own_kernel,
        out_shape=STATE,
        in_specs=[SMEM] + [VMEM] * 3,
        out_specs=[VMEM] * 2,
        scratch_shapes=buffers(PIECES),
        compiler_params=params(16),
    )(table, query_rows, lower, upper)


def more_part(table, query_rows, fill, blocks, state):
    return pl.pallas_call(
        more_kernel,
        out_shape=STATE,
        in_specs=[SMEM] + [VMEM] * (4 + len(blocks)),
        out_specs=[VMEM] * 2,
        scratch_shapes=buffers(2 * PIECES),
        cost_estimate=SMALL,
        compiler_params=params(16),
    )(table, query_rows, fill, *blocks, *state)


def last_part(table, query_rows, fill, blocks, state, kept_local, router, residual):
    return pl.pallas_call(
        last_kernel,
        out_shape=jax.ShapeDtypeStruct((TOK_DEV, HEADS * HD), BF),
        in_specs=[SMEM] + [VMEM] * 9 + [ANY],
        out_specs=ANY,
        scratch_shapes=buffers(PIECES)
        + [pltpu.VMEM(s.shape, s.dtype) for s in STATE]
        + [pltpu.VMEM((TOK_DEV, HEADS * HD), BF)] * 2
        + [pltpu.SemaphoreType.DMA((9,))],
        compiler_params=params(16),
    )(table, query_rows, fill, *blocks, *state, kept_local, router, residual)


def tables(kept_local, y, xl, co):
    own = (y * 2 + xl) * 2 + co
    counts = jnp.sum((kept_local < TOK_DEV).astype(jnp.int32), axis=1)
    at = jnp.arange(4 * PIECES, dtype=jnp.int32)
    group, piece = at // PIECES, at % PIECES
    straight = (piece // 2) ^ (piece // 4)
    split = jnp.where(piece < 4, piece // 2, jnp.where((piece == 4) | (piece == 7), 2, 3))
    behind = jnp.where(group < 2, straight, split)
    half = jnp.where((group < 2) | (piece < 4), piece % 2, jnp.where(piece == 5, 0, piece // 6))
    block = (((y - behind + 4) % 4) * 2 + (xl ^ (group // 2))) * 2 + (co ^ (group % 2))
    block_count = jnp.sum(jnp.where(block[:, None] == jnp.arange(N_CTX), counts[None, :], 0), axis=1)
    live = jnp.where(block < own, jnp.clip(block_count - half * HALF, 0, HALF), 0)
    taken = (live + GRAN - 1) // GRAN * GRAN
    part = (group + 1) // 2
    to = jnp.arange(PIECES_ALL + 3, dtype=jnp.int32)[:, None]
    to_part = jnp.where(to < PIECES_ALL, (to // PIECES + 1) // 2, to - PIECES_ALL)
    counted = (to_part == part[None, :]) & (at[None, :] < to)
    offset = jnp.sum(jnp.where(counted, taken[None, :], 0), axis=1)
    return jnp.concatenate([live, offset, jnp.broadcast_to(own, (1,))]).astype(jnp.int32)


def shards(residual, queries, keys_values, kept_local, router_weight):
    y, xl, co = (lax.axis_index(a) for a in CTX)
    sent = sorted_part(queries, keys_values)
    sent = lax.all_to_all(sent, TP, split_axis=0, concat_axis=0, tiled=True)
    sent = sent.reshape(CAP, (HEADS + 2) * HD)
    query_rows, pairs = sent[:, : HEADS * HD], sent[:, HEADS * HD :]
    table = tables(kept_local, y, xl, co)
    router = jnp.broadcast_to(router_weight[0].astype(F32)[:, None], (CAP, HD))
    pairs, table, router = lax.optimization_barrier((pairs, table, router))

    behind_1, behind_3, behind_2 = (shift(pairs, "y", d) for d in (1, 3, 2))
    own_x = shift_x(pairs, 1)
    lower = jnp.concatenate([pairs, behind_1], axis=0)
    upper = jnp.concatenate([behind_3, behind_2], axis=0)
    lower_x = shift_x(jnp.concatenate([behind_1, behind_2[:HALF]], axis=0), 1)
    upper_x = shift_x(jnp.concatenate([behind_3, behind_2[HALF:]], axis=0), 3)
    state = own_part(table, query_rows, lower, upper)
    low, up, *state = lax.optimization_barrier((lower, upper, *state))
    others = [shift(low, "co", 1), shift(up, "co", 1)]
    own_x, lower_x, upper_x, *state = lax.optimization_barrier((own_x, lower_x, upper_x, *state))
    arrived = [own_x, lower_x, upper_x]
    swapped = [shift(x, "co", 1) for x in arrived]
    state = more_part(table, query_rows, pairs, [*others, *arrived], state)
    return last_part(table, query_rows, pairs, swapped, state, kept_local, router, residual)


def solution(mesh):
    grid = Mesh(mesh.devices.reshape(4, 2, 2, 8, 2), CTX + TP)
    placed = (P(CTX, TP), P(CTX, TP, None), P(CTX, TP, None), P(), P(CTX, None))
    return jax.shard_map(shards, mesh=grid, in_specs=placed, out_specs=P(CTX, TP), check_vma=False)
```
